32 devices in a mesh: groups: 2 (over y), vis: 8 (over z, x), band: 2 (over core).
Axes of the slice: x: 2, y: 2, z: 4, core: 2. Of those that a mesh axis runs over, the one named last changes fastest.
Arguments:
- pieces: bfloat16 [2, 3072, 128, 128], P('band', ('groups', 'vis')), parts along dimension 1, may hold values from -6 to 6
- visit: int32 [2, 3072], P('band', ('groups', 'vis')), parts along dimension 1, may hold values from 0 to 23
- tile_map: int32 [2, 3072, 1], P('band', ('groups', 'vis')), parts along dimension 1, may hold values from 0 to 7; in each aligned block of 192 rows (0 to 191, 192 to 383, ..., all dimensions but the last counted through in order) at most 48 rows name the same one
- good_columns: int32 [2, 3072, 4], P('band', ('groups', 'vis')), parts along dimension 1, may hold values from -2147483648 to 2147483646, as said below
- psf_taps: float32 [2, 3072, 2, 21], P('band', ('groups', 'vis')), parts along dimension 1, may hold values from 0.05 to 1
- shifts: float32 [2, 3072, 2], P('band', ('groups', 'vis')), parts along dimension 1, may hold values from -0.5 to 0.5
- calib: float32 [2, 24], P('band'), may hold values from 0.5 to 2
- weights: int32 [2, 24], P('band'), may hold values from 1 to 8
- band_gain: float32 [2], P('band'), may hold values from 0.5 to 2
Outputs:
- coadd: float32 [2, 2048, 128], P('band', ('groups', 'vis')), parts along dimension 1
- detection: float32 [2048, 128], P(('groups', 'vis')), parts along dimension 0
The draws below stay inside these ranges and needn't reach their ends.
There are 2 independent parts, one for each index of `groups`. The reference program is written for one: setup_inputs(seed, part) draws one part's arguments, and reference() takes and returns one part's arrays. A program takes and returns all parts, laid end to end along the dimension named above; an argument that names none is the same for every part. Nothing has to cross between parts.
Inputs may be any that keep to these rules, and one draw needn't show every extreme that they name: `tile_map`: among the 192 pieces of one band on one index of vis (aligned blocks of 192 pieces), no tile appears more than 48 times, a bound that some block reaches. `good_columns`: independent random bits.
All inputs are finite; a program needn't handle non-finite values.
Results may differ from the reference program's by a relative error of at most 0.0081.
Values may be sent and summed in bfloat16 or wider, within the bound.
A program may use at most 128 MiB of HBM per device.

```python
import math
import jax
import jax.numpy as jnp
import numpy as np
from jax import lax

PIX = 128
PD = 192
VISITS = 24
KT = 21
BANDS = 2
TILES = 8
PIECES = 1536
WORDS = 4
CAP = 48
N_VIS = 8


def draw_good_columns(key, part):
    return jax.random.randint(key, (BANDS, PIECES, WORDS), -2147483648, 2147483647, dtype=jnp.int32)


def set_ends(values, key, least, top_value):
    longest = values.shape.index(max(values.shape))
    spots = []
    for shift in (0, 1):
        where = [jax.random.randint(jax.random.fold_in(key, axis), (), 0, length) for axis, length in enumerate(values.shape)]
        where[longest] = (where[longest] + shift) % values.shape[longest]
        spots.append(tuple(where))
    return values.at[spots[0]].set(least).at[spots[1]].set(top_value)


def block_levels(rng, dims, cuts, least, largest):
    level, own = 1.0, jax.random.fold_in(rng, 6)
    for dim, blocks in cuts:
        draws = jnp.exp(jax.random.uniform(jax.random.fold_in(own, dim), (blocks,), jnp.float32, least / len(cuts), largest / len(cuts)))
        level = level * jnp.repeat(draws, dims[dim] // blocks).reshape([-1 if axis == dim else 1 for axis in range(len(dims))])
    return level


def assign_block(own_key, own, number, rows, amount, top, bound, lean):
    ranking = jax.random.permutation(own_key, amount)
    crowded, usual = portions_of(amount, rows * top, bound, lean, True), portions_of(amount, rows * top, bound, lean, False)
    places = jnp.arange(amount)

    def named(sizes, rotation):
        used = int((sizes > 0).sum())
        fixed = max(1, used // 4)
        passed = fixed + (places - fixed + rotation * (used - fixed)) % max(1, amount - fixed)
        return jnp.zeros((amount,), jnp.int32).at[ranking[jnp.where(places < fixed, places, passed)]].set(jnp.asarray(sizes, jnp.int32))

    sizes = jnp.where(number % 4 == 0, named(crowded, number // 4), named(usual, number - number // 4 - 1))
    mixed = jax.random.permutation(jax.random.fold_in(own, 3), amount)
    donor, sink = mixed[0:amount // 2 * 2:2], mixed[1:amount // 2 * 2:2]
    room = jnp.minimum(sizes[donor] - 1, bound - sizes[sink]) // 2
    room = jnp.where((donor == ranking[0]) | (sink == ranking[0]) | (sizes[sink] == 0), 0, jnp.maximum(room, 0))
    passed = jax.random.randint(jax.random.fold_in(own, 4), (amount // 2,), 0, 1 << 20) % (room + 1)
    sizes = sizes.at[donor].add(-passed).at[sink].add(passed)
    members = jnp.searchsorted(jnp.cumsum(sizes), jnp.arange(rows * top), side="right").astype(jnp.int32)
    table = members.reshape(top, rows).T
    table = table[jax.random.permutation(jax.random.fold_in(own, 1), rows)]
    rotation = jax.random.randint(jax.random.fold_in(own, 2), (rows, 1), 0, top)
    return jnp.take_along_axis(table, (jnp.arange(top)[None, :] + rotation) % top, axis=1)


def portions_of(amount, total, most, skew, full):
    weights = [(1 << 20) // math.isqrt(rank ** skew) + 1 for rank in range(1, amount + 1)]
    largest = most if full else min(most, max(-(-total // amount), total * weights[0] // sum(weights)))
    least = 1 if total - largest >= amount - 1 else 0
    holding, spare = [largest] + [least] * (amount - 1), total - largest - least * (amount - 1)
    while spare > 0:
        free = [i for i in range(1, amount) if holding[i] < largest] or [i for i in range(1, amount) if holding[i] < most]
        pool, budget = sum([weights[i] for i in free]), spare
        for i in free:
            addition = min(most - holding[i], max(1, budget * weights[i] // pool), spare)
            holding[i] = holding[i] + addition
            spare = spare - addition
    return np.array(holding)


def bell_draw(rng, dims, deviation, most, shards=(), held_as=jnp.bfloat16):
    level = block_levels(rng, dims, shards, -0.22, 0.18) if shards else 1.0
    values = jax.random.normal(rng, dims, jnp.float32) * deviation * level
    return jnp.minimum(jnp.maximum(values, -most), most).astype(held_as)


def setup_inputs(seed: int = 0, part: int = 0) -> dict:
    arg_keys = jax.random.split(jax.random.key(seed), 10)
    own_keys = jax.random.split(jax.random.fold_in(arg_keys[9], part), 10)
    pieces = bell_draw(own_keys[0], (BANDS, PIECES, PIX, PIX), 1.0, 6.0, ((0, 2), (1, 8)))
    visit = set_ends(jax.random.randint(own_keys[1], (BANDS, PIECES), 0, VISITS), jax.random.fold_in(own_keys[1], 1), 0, VISITS - 1).astype(jnp.int32)
    tile_map_keys = jax.random.split(jax.random.fold_in(own_keys[2], 1), BANDS * PIECES // PD)
    tile_map_turns = jax.random.permutation(jax.random.fold_in(own_keys[2], 3), BANDS * PIECES // PD)
    tile_map = jax.vmap(lambda own, number: assign_block(jax.random.fold_in(own_keys[2], 2), own, number, PD, TILES, 1, CAP, 2))(tile_map_keys, tile_map_turns).reshape((BANDS, PIECES, 1))
    good_columns = draw_good_columns(jax.random.fold_in(jax.random.fold_in(arg_keys[9], part), 71), part)
    psf_taps = jnp.clip(jnp.exp(math.log(1.0) - 2.9957323 * jax.random.uniform(own_keys[4], (BANDS, PIECES, 2, KT), jnp.float32) ** block_levels(own_keys[4], (BANDS, PIECES, 2, KT), ((0, 2), (1, 8)), -0.2, 0.2)), 0.05, 1.0)
    shifts = jnp.clip(jax.random.uniform(own_keys[5], (BANDS, PIECES, 2), jnp.float32, -0.5, 0.5) * block_levels(own_keys[5], (BANDS, PIECES, 2), ((0, 2), (1, 8)), -0.4, 0.0), -0.5, 0.5)
    calib = jnp.clip(jnp.exp(math.log(2.0) - 1.3862944 * jax.random.uniform(arg_keys[6], (BANDS, VISITS), jnp.float32) ** block_levels(arg_keys[6], (BANDS, VISITS), ((0, 2),), -0.2, 0.2)), 0.5, 2.0)
    weights = set_ends(jax.random.randint(arg_keys[7], (BANDS, VISITS), 1, 9), jax.random.fold_in(arg_keys[7], 1), 1, 8).astype(jnp.int32)
    band_gain = jnp.clip(jnp.exp(math.log(2.0) - 1.3862944 * jax.random.uniform(arg_keys[8], (BANDS,), jnp.float32) ** block_levels(arg_keys[8], (BANDS,), ((0, 2),), -0.2, 0.2)), 0.5, 2.0)
    return {"pieces": pieces, "visit": visit, "tile_map": tile_map, "good_columns": good_columns, "psf_taps": psf_taps, "shifts": shifts, "calib": calib, "weights": weights, "band_gain": band_gain}


def good_mask(words):
    bits = jnp.arange(32, dtype=jnp.int32)
    flags = jnp.right_shift(words[..., None], bits) & 1
    return flags.reshape(words.shape[:-1] + (words.shape[-1] * 32,)).astype(jnp.float32)


def kernel_matrix(taps, size):
    kernel = taps / jnp.sum(taps, axis=-1, keepdims=True)
    reach = (taps.shape[-1] - 1) // 2
    result = jnp.zeros((taps.shape[0], size, size), jnp.float32)
    for tap in range(taps.shape[-1]):
        result = result + kernel[:, tap, None, None] * jnp.eye(size, k=tap - reach, dtype=jnp.float32)
    return result.astype(jnp.bfloat16)


def lanczos(values):
    inside = jnp.abs(values) < 3.0
    return jnp.where(inside, jnp.sinc(values) * jnp.sinc(values / 3.0), 0.0)


def warp_matrix(offset, size):
    places = jnp.arange(size).astype(jnp.float32)
    spread = places[None, None, :] - places[None, :, None] - offset[:, None, None]
    steps = jnp.arange(-3, 4).astype(jnp.float32)
    norms = jnp.sum(lanczos(steps[None, :] - offset[:, None]), axis=1)
    return (lanczos(spread) / norms[:, None, None]).astype(jnp.bfloat16)


def warp_pieces(pieces, visit, words, taps, shifts, calib, weights):
    size = pieces.shape[-1]
    good = good_mask(words)
    match = (visit[:, None] == jnp.arange(calib.shape[0], dtype=jnp.int32)[None, :]).astype(jnp.float32)
    scale = jnp.dot(match, calib, precision=lax.Precision.HIGHEST)
    weight = jnp.sum(match * weights.astype(jnp.float32)[None, :], axis=1)
    calibrated = (pieces.astype(jnp.float32) * scale[:, None, None] * good[:, None, :]).astype(jnp.bfloat16)
    w_rows = warp_matrix(shifts[:, 0], size).astype(jnp.float32)
    w_cols = warp_matrix(shifts[:, 1], size).astype(jnp.float32)
    k_rows = kernel_matrix(taps[:, 0], size).astype(jnp.float32)
    k_cols = kernel_matrix(taps[:, 1], size).astype(jnp.float32)
    left = jnp.einsum('pij,pjk->pik', w_rows, k_rows).astype(jnp.bfloat16)
    right = jnp.einsum('pij,pjk->pik', w_cols, k_cols).astype(jnp.bfloat16)
    inner = jnp.einsum('pij,pkj->pik', calibrated.astype(jnp.float32), right.astype(jnp.float32)).astype(jnp.bfloat16)
    warped = jnp.einsum('pij,pjk->pik', left.astype(jnp.float32), inner.astype(jnp.float32))
    num_piece = (warped * weight[:, None, None]).astype(jnp.bfloat16)
    row_weight = (jnp.sum(left.astype(jnp.float32), axis=2) * weight[:, None]).astype(jnp.bfloat16)
    col_good = jnp.einsum('pij,pj->pi', right.astype(jnp.float32), good).astype(jnp.bfloat16)
    return num_piece, row_weight, col_good


def reference(pieces, visit, tile_map, good_columns, psf_taps, shifts, calib, weights, band_gain):
    coadds = []
    detection = jnp.zeros((TILES * PIX, PIX), jnp.float32)
    for band in range(BANDS):
        def block(items):
            return warp_pieces(items[0], items[1], items[2], items[3], items[4], calib[band], weights[band])

        blocks = (pieces[band].reshape(N_VIS, PD, PIX, PIX), visit[band].reshape(N_VIS, PD),
                  good_columns[band].reshape(N_VIS, PD, WORDS), psf_taps[band].reshape(N_VIS, PD, 2, KT),
                  shifts[band].reshape(N_VIS, PD, 2))
        num_piece, row_weight, col_good = lax.map(block, blocks)
        num_piece = num_piece.reshape(PIECES, PIX, PIX)
        row_weight = row_weight.reshape(PIECES, PIX).astype(jnp.float32)
        col_good = col_good.reshape(PIECES, PIX).astype(jnp.float32)
        tile = tile_map[band, :, 0]
        num = jax.ops.segment_sum(num_piece.astype(jnp.float32), tile, num_segments=TILES)
        onehot = (tile[:, None] == jnp.arange(TILES, dtype=jnp.int32)[None, :]).astype(jnp.float32)

        def tile_den(column):
            return jnp.dot((row_weight * column[:, None]).T, col_good, precision=lax.Precision.HIGHEST)

        den = lax.map(tile_den, onehot.T)
        coadd = (num / jnp.maximum(den, 1.0)).reshape(TILES * PIX, PIX)
        coadds.append(coadd)
        detection = detection + band_gain[band] * coadd
    return jnp.stack(coadds, axis=0), detection
```

```python
import functools
import math

import jax
import jax.numpy as jnp
from jax import lax
from jax.experimental import pallas as pl
from jax.experimental.pallas import tpu as pltpu
from jax.sharding import PartitionSpec as P

GROUP = 4
SIDE = 3
EDGE = 16
MESH = pl.DeviceIdType.MESH


def lanczos(x):
    inside = jnp.abs(x) < 3.0
    u = jnp.where(inside, x, 0.0) * (math.pi / 3.0)
    square = u * u
    q = jnp.full_like(square, -1.0 / math.factorial(23))
    for k in range(10, -1, -1):
        q = q * square + (-1.0 if k % 2 else 1.0) / math.factorial(2 * k + 1)
    q2 = q * q
    return jnp.where(inside, q2 * (1.0 - (4.0 / 3.0) * square * q2), 0.0)


def tap_rows(taps, shift, size):
    rows, count = taps.shape
    reach = (count - 1) // 2
    lane = lax.broadcasted_iota(jnp.int32, (rows, size), 1)
    k = taps / jnp.sum(taps, axis=1, keepdims=True)
    k = jnp.concatenate([k, jnp.zeros((rows, size - count), jnp.float32)], axis=1)
    k = k.astype(jnp.bfloat16).astype(jnp.float32)
    w = lanczos((lane - SIDE).astype(jnp.float32) - shift)
    w = jnp.where(lane <= 2 * SIDE, w, 0.0)
    w = w / jnp.sum(w, axis=1, keepdims=True)
    w = w.astype(jnp.bfloat16).astype(jnp.float32)
    terms = [
        w[:, m + SIDE : m + SIDE + 1] * pltpu.roll(k, (m - reach) % size, 1)
        for m in range(-SIDE, SIDE + 1)
    ]
    down = terms[6] + terms[5] + terms[4]
    first = []
    for m in range(SIDE, -1, -1):
        down = down + terms[m]
        first.append(down)
    up = terms[0] + terms[1] + terms[2]
    last = []
    for m in range(SIDE, 2 * SIDE):
        up = up + terms[m]
        last.append(up)
    return first + last


def band_matrix(ref, p, size, masks):
    sub, keep = masks
    row = [jnp.broadcast_to(ref[v, pl.ds(p, 1), :], (8, size)) for v in range(7)]
    top = jnp.where(sub == 0, row[0], jnp.where(sub == 1, row[1], jnp.where(sub == 2, row[2], row[3])))
    end = jnp.where(sub == 7, row[4], jnp.where(sub == 6, row[5], jnp.where(sub == 5, row[6], row[3])))
    base = pltpu.roll(row[3], 0, 1, stride=1, stride_axis=0)
    parts = []
    tiles = size // 8
    for v in range(tiles):
        if v == 0:
            x = pltpu.roll(top, 0, 1, stride=1, stride_axis=0)
        elif v == tiles - 1:
            x = pltpu.roll(end, size - 8, 1, stride=1, stride_axis=0)
        else:
            x = pltpu.roll(base, 8 * v, 1)
        if v in keep:
            x = jnp.where(keep[v], x, 0.0)
        parts.append(x)
    return [
        jnp.concatenate(parts[2 * v : 2 * v + 2], axis=0).astype(jnp.bfloat16)
        for v in range(tiles // 2)
    ]


def sums_kernel(
    tile_ref, visit_ref, calib_ref, weights_ref, words_ref, taps_ref, shifts_ref, pieces_ref,
    out_ref,
    pbuf, left_taps, right_taps, good, acc, dacc, lbuf, rbuf, ibuf, cbuf,
    slots, blk_tile, cnt, cur, sems,
):
    count, size, _ = pieces_ref.shape
    tiles = acc.shape[0]
    chunks = sems.shape[0]
    each = count // chunks
    copies = [
        pltpu.make_async_copy(
            pieces_ref.at[pl.ds(c * each, each)], pbuf.at[pl.ds(c * each, each)], sems.at[c]
        )
        for c in range(chunks)
    ]
    for copy in copies:
        copy.start()

    def clear_slot(i, carry):
        slots[i] = -1
        return carry

    lax.fori_loop(0, slots.shape[0], clear_slot, 0, unroll=8)

    def clear_blk(i, carry):
        blk_tile[i] = 0
        return carry

    lax.fori_loop(0, blk_tile.shape[0], clear_blk, 0, unroll=8)
    for t in range(tiles):
        cnt[t] = 0
        cur[t] = 0
        acc[t] = jnp.zeros((size, size), jnp.float32)
        dacc[t] = jnp.zeros((2 * EDGE, size), jnp.float32)
    lbuf[...] = jnp.zeros_like(lbuf)
    ibuf[...] = jnp.zeros_like(ibuf)
    cbuf[...] = jnp.zeros_like(cbuf)

    words = words_ref.shape[1]
    lane8 = lax.broadcasted_iota(jnp.int32, (8, size), 1)

    def prepare(c, used):
        start = pl.multiple_of(c * 8, 8)
        here = pl.ds(start, 8)
        for i in range(8):
            t = tile_ref[start + i]
            n = cnt[t]
            inside = n & (GROUP - 1)
            fresh = inside == 0
            b = jnp.where(fresh, used, cur[t])
            cur[t] = b
            blk_tile[b + 1] = t
            slots[b * GROUP + inside] = start + i
            cnt[t] = n + 1
            used = jnp.where(fresh, used + 1, used)
        for d, table in ((0, left_taps), (1, right_taps)):
            rows = tap_rows(taps_ref[here, d, :], shifts_ref[here, d : d + 1], size)
            for v in range(7):
                table[v, here, :] = rows[v]
        packed = words_ref[here, :]
        word = jnp.broadcast_to(packed[:, 0:1], (8, size))
        for k in range(1, words):
            word = jnp.where(lane8 >= 32 * k, packed[:, k : k + 1], word)
        bit = lax.shift_right_logical(word, lane8 & 31) & 1
        good[here, :] = bit.astype(jnp.float32)
        return used

    used = lax.fori_loop(0, count // 8, prepare, jnp.int32(0))

    sub = lax.broadcasted_iota(jnp.int32, (8, size), 0)
    gap = lane8 - sub
    reach = (taps_ref.shape[2] - 1) // 2 + SIDE
    last = size // 8 - 1
    keep = {v: jnp.abs(gap - 8 * v) <= reach for v in (0, 1, last - 1, last)}
    masks = (sub, keep)

    def piece_of(step, g):
        return jnp.maximum(slots[step * GROUP + g], 0)

    def weight_of(step, g):
        p = slots[step * GROUP + g]
        v = visit_ref[jnp.maximum(p, 0)]
        w = jnp.where(p >= 0, weights_ref[v], 0).astype(jnp.float32)
        return w, w * calib_ref[v]

    def build_right(step):
        for g in range(GROUP):
            p = piece_of(step, g)
            mask = jnp.broadcast_to(good[pl.ds(p, 1), :], (16, size)).astype(jnp.bfloat16)
            parts = band_matrix(right_taps, p, size, masks)
            for v, part in enumerate(parts):
                rbuf[g, 16 * v : 16 * v + 16, :] = part * mask

    def build_left(step):
        for g in range(GROUP):
            p = piece_of(step, g)
            parts = band_matrix(left_taps, p, size, masks)
            for v, part in enumerate(parts):
                lbuf[16 * v : 16 * v + 16, g * size : (g + 1) * size] = part

    for copy in copies:
        copy.wait()
    build_right(0)
    ones = jnp.ones((16, size), jnp.bfloat16)

    def step_body(k, carry):
        t = blk_tile[k]
        part = jnp.dot(lbuf[...], ibuf[...], preferred_element_type=jnp.float32)
        acc[t] = acc[t] + part
        den = dacc[t]
        for g in range(GROUP):
            cols = slice(g * size, (g + 1) * size)
            rim = jnp.concatenate(
                [lbuf[0:EDGE, cols], lbuf[size - EDGE : size, cols]], axis=0
            ).astype(jnp.float32)
            den = den + jnp.sum(rim, axis=1, keepdims=True) * cbuf[g, 0:1, :]
        dacc[t] = den
        for g in range(GROUP):
            p = piece_of(k, g)
            w, factor = weight_of(k, g)
            x = jnp.concatenate([pbuf[p], ones], axis=0)
            y = lax.dot_general(
                x, rbuf[g], (((1,), (1,)), ((), ())), preferred_element_type=jnp.float32
            )
            ibuf[g * size : (g + 1) * size, :] = (y[0:size] * factor).astype(jnp.bfloat16)
            cbuf[g] = y[size : size + 8] * w
        build_left(k)
        build_right(k + 1)
        return carry

    lax.fori_loop(0, used + 1, step_body, 0)
    for t in range(tiles):
        out_ref[t, 0:size, :] = acc[t].astype(jnp.bfloat16)
        out_ref[t, size : size + 2 * EDGE, :] = dacc[t].astype(jnp.bfloat16)


def local_sums(pieces, visit, tile, words, taps, shifts, calib, weights, tiles):
    count, size, _ = pieces.shape
    blocks = (count + tiles * (GROUP - 1)) // GROUP + 2
    smem = pl.BlockSpec(memory_space=pltpu.SMEM)
    vmem = pl.BlockSpec(memory_space=pltpu.VMEM)
    chunks = 8 if count % 8 == 0 else 1
    return pl.pallas_call(
        sums_kernel,
        out_shape=jax.ShapeDtypeStruct((tiles, size + 2 * EDGE, size), jnp.bfloat16),
        in_specs=[smem] * 4 + [vmem] * 3 + [pl.BlockSpec(memory_space=pl.ANY)],
        out_specs=vmem,
        scratch_shapes=[
            pltpu.VMEM((count, size, size), jnp.bfloat16),
            pltpu.VMEM((7, count, size), jnp.float32),
            pltpu.VMEM((7, count, size), jnp.float32),
            pltpu.VMEM((count, size), jnp.float32),
            pltpu.VMEM((tiles, size, size), jnp.float32),
            pltpu.VMEM((tiles, 2 * EDGE, size), jnp.float32),
            pltpu.VMEM((size, GROUP * size), jnp.bfloat16),
            pltpu.VMEM((GROUP, size, size), jnp.bfloat16),
            pltpu.VMEM((GROUP * size, size), jnp.bfloat16),
            pltpu.VMEM((GROUP, 8, size), jnp.float32),
            pltpu.SMEM((blocks * GROUP,), jnp.int32),
            pltpu.SMEM((blocks + 1,), jnp.int32),
            pltpu.SMEM((tiles,), jnp.int32),
            pltpu.SMEM((tiles,), jnp.int32),
            pltpu.SemaphoreType.DMA((chunks,)),
        ],
        compiler_params=pltpu.CompilerParams(vmem_limit_bytes=40 * 1024 * 1024),
        name="local_sums",
    )(tile, visit, calib, weights, words, taps, shifts, pieces)


def owner_kernel(
    owners, bands, gain_ref, sums_ref, coadd_ref, det_ref,
    got, mine, other, send_sem, recv_sem, band_send, band_recv,
):
    size = coadd_ref.shape[0]
    me = lax.axis_index("vis")
    band = lax.axis_index("band")
    barrier = pltpu.get_barrier_semaphore()
    for o in range(1, owners):
        pl.semaphore_signal(
            barrier, inc=1, device_id={"vis": lax.rem(me + o, owners)}, device_id_type=MESH
        )
    for o in range(1, bands):
        pl.semaphore_signal(
            barrier, inc=1, device_id={"band": lax.rem(band + o, bands)}, device_id_type=MESH
        )
    pl.semaphore_wait(barrier, owners + bands - 2)
    copies = []
    for o in range(1, owners):
        to = lax.rem(me + o, owners)
        copy = pltpu.make_async_remote_copy(
            src_ref=sums_ref.at[to],
            dst_ref=got.at[o],
            send_sem=send_sem.at[o],
            recv_sem=recv_sem.at[o],
            device_id={"vis": to},
            device_id_type=MESH,
        )
        copy.start()
        copies.append(copy)
    total = sums_ref[me].astype(jnp.float32)
    for o in range(1, owners):
        copies[o - 1].wait_recv()
        total = total + got[o].astype(jnp.float32)
    num = total[0:size]
    rim = jnp.maximum(total[size:], 1.0)
    inner = jnp.broadcast_to(rim[EDGE - 1 : EDGE], (size - 2 * EDGE, size))
    den = jnp.concatenate([rim[:EDGE], inner, rim[EDGE:]], axis=0)
    coadd = num / den
    coadd_ref[...] = coadd
    scaled = coadd * gain_ref[0]
    mine[...] = scaled
    swaps = []
    for o in range(1, bands):
        swap = pltpu.make_async_remote_copy(
            src_ref=mine,
            dst_ref=other.at[o],
            send_sem=band_send.at[o],
            recv_sem=band_recv.at[o],
            device_id={"band": lax.rem(band + o, bands)},
            device_id_type=MESH,
        )
        swap.start()
        swaps.append(swap)
    for o in range(1, bands):
        swaps[o - 1].wait_recv()
        scaled = scaled + other[o]
    det_ref[...] = scaled
    for copy in copies + swaps:
        copy.wait_send()


def owner_coadd(gain, sums, owners, bands):
    tiles, rows, size = sums.shape
    vmem = pl.BlockSpec(memory_space=pltpu.VMEM)
    out = jax.ShapeDtypeStruct((size, size), jnp.float32)
    return pl.pallas_call(
        functools.partial(owner_kernel, owners, bands),
        out_shape=(out, out),
        in_specs=[pl.BlockSpec(memory_space=pltpu.SMEM), vmem],
        out_specs=(vmem, vmem),
        scratch_shapes=[
            pltpu.VMEM((owners, rows, size), jnp.bfloat16),
            pltpu.VMEM((size, size), jnp.float32),
            pltpu.VMEM((bands, size, size), jnp.float32),
            pltpu.SemaphoreType.DMA((owners,)),
            pltpu.SemaphoreType.DMA((owners,)),
            pltpu.SemaphoreType.DMA((bands,)),
            pltpu.SemaphoreType.DMA((bands,)),
        ],
        compiler_params=pltpu.CompilerParams(
            collective_id=0, has_side_effects=True, vmem_limit_bytes=32 * 1024 * 1024
        ),
        name="owner_coadd",
    )(gain, sums)


def shards(pieces, visit, tile_map, good_columns, psf_taps, shifts, calib, weights, band_gain):
    owners = lax.axis_size("vis")
    sums = local_sums(
        pieces[0], visit[0], tile_map[0, :, 0], good_columns[0], psf_taps[0], shifts[0],
        calib[0], weights[0], owners,
    )
    coadd, detection = owner_coadd(band_gain, sums, owners, lax.axis_size("band"))
    return (coadd[None], detection)


def solution(mesh):
    placed = (
        P("band", ("groups", "vis"), None, None),
        P("band", ("groups", "vis")),
        P("band", ("groups", "vis"), None),
        P("band", ("groups", "vis"), None),
        P("band", ("groups", "vis"), None, None),
        P("band", ("groups", "vis"), None),
        P("band", None),
        P("band", None),
        P("band"),
    )
    return jax.shard_map(
        shards,
        mesh=mesh,
        in_specs=placed,
        out_specs=(P("band", ("groups", "vis"), None), P(("groups", "vis"), None)),
        check_vma=False,
    )
```

```python
import functools
import math

import jax
import jax.numpy as jnp
from jax import lax
from jax.experimental import pallas as pl
from jax.experimental.pallas import tpu as pltpu
from jax.sharding import PartitionSpec as P

GROUP = 4
SIDE = 3
EDGE = 16
MESH = pl.DeviceIdType.MESH


def lanczos(x):
    inside = jnp.abs(x) < 3.0
    u = jnp.where(inside, x, 0.0) * (math.pi / 3.0)
    square = u * u
    q = jnp.full_like(square, -1.0 / math.factorial(23))
    for k in range(10, -1, -1):
        q = q * square + (-1.0 if k % 2 else 1.0) / math.factorial(2 * k + 1)
    q2 = q * q
    return jnp.where(inside, q2 * (1.0 - (4.0 / 3.0) * square * q2), 0.0)


def tap_columns(padded, shift, width):
    sub = lax.broadcasted_iota(jnp.int32, (8, shift.shape[1]), 0)
    w = lanczos((sub - SIDE).astype(jnp.float32) - shift)
    w = jnp.where(sub <= 2 * SIDE, w, 0.0)
    w = w / jnp.sum(w, axis=0, keepdims=True)
    w = w.astype(jnp.bfloat16).astype(jnp.float32)
    terms = [
        w[m + SIDE : m + SIDE + 1] * padded[SIDE - m : SIDE - m + width, :]
        for m in range(-SIDE, SIDE + 1)
    ]
    down = terms[6] + terms[5] + terms[4]
    first = []
    for m in range(SIDE, -1, -1):
        down = down + terms[m]
        first.append(down)
    up = terms[0] + terms[1] + terms[2]
    last = []
    for m in range(SIDE, 2 * SIDE):
        up = up + terms[m]
        last.append(up)
    return first, last


def band_matrix(ref, p, size, masks):
    sub, keep = masks
    row = [jnp.broadcast_to(ref[v, pl.ds(p, 1), :], (8, size)) for v in range(7)]
    top = jnp.where(sub == 0, row[0], jnp.where(sub == 1, row[1], jnp.where(sub == 2, row[2], row[3])))
    end = jnp.where(sub == 7, row[4], jnp.where(sub == 6, row[5], jnp.where(sub == 5, row[6], row[3])))
    base = pltpu.roll(row[3], 0, 1, stride=1, stride_axis=0)
    top = pltpu.roll(top, 0, 1, stride=1, stride_axis=0)
    end = pltpu.roll(end, size - 8, 1, stride=1, stride_axis=0)
    tiles = size // 8
    next8 = pltpu.roll(base, 8, 1)
    head = [jnp.where(keep[0], top, 0.0), jnp.where(keep[1], next8, 0.0)]
    tail = [
        jnp.where(keep[tiles - 2], pltpu.roll(base, size - 16, 1), 0.0),
        jnp.where(keep[tiles - 1], end, 0.0),
    ]
    pair = jnp.concatenate([base, next8], axis=0).astype(jnp.bfloat16)
    parts = [jnp.concatenate(head, axis=0).astype(jnp.bfloat16)]
    for v in range(1, tiles // 2 - 1):
        parts.append(pltpu.roll(pair, 16 * v, 1))
    parts.append(jnp.concatenate(tail, axis=0).astype(jnp.bfloat16))
    return parts


def sums_kernel(
    tile_hbm, visit_hbm, calib_hbm, weights_hbm, words_hbm, taps_hbm, shifts_hbm, pieces_ref,
    out_ref,
    pbuf, words_ref, taps_ref, shifts_ref, padded, columns, left_taps, right_taps, good,
    acc, dacc, lbuf, rbuf, ibuf, cbuf,
    tile_ref, visit_ref, calib_ref, weights_ref, slots, blk_tile, cnt, cur, sems, small_sems,
):
    count, size, _ = pieces_ref.shape
    tiles = acc.shape[0]
    chunks = sems.shape[0]
    each = count // chunks
    smalls = [
        pltpu.make_async_copy(src, dst, small_sems.at[i])
        for i, (src, dst) in enumerate(
            (
                (tile_hbm, tile_ref), (shifts_hbm, shifts_ref), (taps_hbm, taps_ref),
                (words_hbm, words_ref), (visit_hbm, visit_ref), (calib_hbm, calib_ref),
                (weights_hbm, weights_ref),
            )
        )
    ]
    for copy in smalls:
        copy.start()
    copies = [
        pltpu.make_async_copy(
            pieces_ref.at[pl.ds(c * each, each)], pbuf.at[pl.ds(c * each, each)], sems.at[c]
        )
        for c in range(chunks)
    ]
    for copy in copies:
        copy.start()

    def clear_slot(i, carry):
        slots[i] = -1
        return carry

    lax.fori_loop(0, slots.shape[0], clear_slot, 0, unroll=8)

    def clear_blk(i, carry):
        blk_tile[i] = 0
        return carry

    lax.fori_loop(0, blk_tile.shape[0], clear_blk, 0, unroll=8)
    for t in range(tiles):
        cnt[t] = 0
        cur[t] = 0
        acc[t] = jnp.zeros((size, size), jnp.float32)
        dacc[t] = jnp.zeros((2 * EDGE, size), jnp.float32)
    lbuf[...] = jnp.zeros_like(lbuf)
    ibuf[...] = jnp.zeros_like(ibuf)
    cbuf[...] = jnp.zeros_like(cbuf)
    padded[...] = jnp.zeros_like(padded)
    for copy in smalls:
        copy.wait()

    def place(i, used):
        t = tile_ref[0, i]
        n = cnt[t]
        inside = n & (GROUP - 1)
        fresh = inside == 0
        b = jnp.where(fresh, used, cur[t])
        cur[t] = b
        blk_tile[b + 1] = t
        slots[b * GROUP + inside] = i
        cnt[t] = n + 1
        return jnp.where(fresh, used + 1, used)

    used = lax.fori_loop(0, count, place, jnp.int32(0), unroll=8)

    taps_count = taps_ref.shape[0]
    reach = (taps_count - 1) // 2 + SIDE
    block = size // 4
    wide = padded.shape[2]
    place_lane = lax.broadcasted_iota(jnp.int32, (size, size), 1)
    inside = (place_lane < block - reach) | (place_lane >= size - reach)
    for d, table in ((0, left_taps), (1, right_taps)):
        taps = taps_ref[:, d, :]
        kernel = taps / jnp.sum(taps, axis=0, keepdims=True)
        kernel = kernel.astype(jnp.bfloat16).astype(jnp.float32)
        padded[d, 2 * SIDE : 2 * SIDE + taps_count, 0:count] = kernel
        shift = jnp.concatenate(
            [shifts_ref[d : d + 1, :], jnp.zeros((1, wide - count), jnp.float32)], axis=1
        )
        first, last = tap_columns(padded.at[d], shift, block)
        for v, rows in enumerate(first):
            columns[0, block * v : block * (v + 1), :] = rows
        for v, rows in enumerate(last):
            columns[1, block * v : block * (v + 1), :] = rows
        columns[1, 3 * block : size, :] = first[3]
        for h in range(2):
            for c in range(wide // size):
                part = columns[h, :, c * size : (c + 1) * size]
                turned = part.T
                for v in range(4 if h == 0 else 3):
                    x = pltpu.roll(turned, (-block * v - reach) % size, 1)
                    table[4 * h + v, c * size : (c + 1) * size, :] = jnp.where(inside, x, 0.0)
    bit = lax.broadcasted_iota(jnp.int32, (32, count), 0)
    flags = [
        (lax.shift_right_logical(jnp.broadcast_to(words_ref[k : k + 1, :], (32, count)), bit) & 1)
        for k in range(size // 32)
    ]
    columns[0, :, 0:count] = jnp.concatenate(flags, axis=0).astype(jnp.float32)
    for c in range(wide // size):
        good[c * size : (c + 1) * size, :] = columns[0, :, c * size : (c + 1) * size].T

    sub = lax.broadcasted_iota(jnp.int32, (8, size), 0)
    lane = lax.broadcasted_iota(jnp.int32, (8, size), 1)
    final = size // 8 - 1
    keep = {v: jnp.abs(lane - sub - 8 * v) <= reach for v in (0, 1, final - 1, final)}
    masks = (sub, keep)

    def piece_of(step, g):
        return jnp.maximum(slots[step * GROUP + g], 0)

    def weight_of(step, g):
        p = slots[step * GROUP + g]
        v = visit_ref[0, jnp.maximum(p, 0)]
        w = jnp.where(p >= 0, weights_ref[0, v], 0).astype(jnp.float32)
        return w, w * calib_ref[0, v]

    def build_right(step):
        for g in range(GROUP):
            p = piece_of(step, g)
            mask = jnp.broadcast_to(good[pl.ds(p, 1), :], (16, size)).astype(jnp.bfloat16)
            parts = band_matrix(right_taps, p, size, masks)
            for v, part in enumerate(parts):
                rbuf[g, 16 * v : 16 * v + 16, :] = part * mask

    def build_left(step):
        for g in range(GROUP):
            p = piece_of(step, g)
            parts = band_matrix(left_taps, p, size, masks)
            for v, part in enumerate(parts):
                lbuf[16 * v : 16 * v + 16, g * size : (g + 1) * size] = part

    for copy in copies:
        copy.wait()
    build_right(0)
    ones = jnp.ones((16, size), jnp.bfloat16)

    def step_body(k, carry):
        t = blk_tile[k]
        part = jnp.dot(lbuf[...], ibuf[...], preferred_element_type=jnp.float32)
        acc[t] = acc[t] + part
        den = dacc[t]
        for g in range(GROUP):
            cols = slice(g * size, (g + 1) * size)
            rim = jnp.concatenate(
                [lbuf[0:EDGE, cols], lbuf[size - EDGE : size, cols]], axis=0
            ).astype(jnp.float32)
            den = den + jnp.sum(rim, axis=1, keepdims=True) * cbuf[g, 0:1, :]
        dacc[t] = den
        for g in range(GROUP):
            p = piece_of(k, g)
            w, factor = weight_of(k, g)
            x = jnp.concatenate([pbuf[p], ones], axis=0)
            y = lax.dot_general(
                x, rbuf[g], (((1,), (1,)), ((), ())), preferred_element_type=jnp.float32
            )
            ibuf[g * size : (g + 1) * size, :] = (y[0:size] * factor).astype(jnp.bfloat16)
            cbuf[g] = y[size : size + 8] * w
        build_left(k)
        build_right(k + 1)
        return carry

    lax.fori_loop(0, used + 1, step_body, 0)
    for t in range(tiles):
        out_ref[t, 0:size, :] = acc[t].astype(jnp.bfloat16)
        out_ref[t, size : size + 2 * EDGE, :] = dacc[t].astype(jnp.bfloat16)


def local_sums(pieces, visit, tile, words, taps, shifts, calib, weights, tiles):
    count, size, _ = pieces.shape
    blocks = (count + tiles * (GROUP - 1)) // GROUP + 2
    hbm = pl.BlockSpec(memory_space=pltpu.HBM)
    chunks = 8 if count % 8 == 0 else 1
    wide = -(-count // size) * size
    return pl.pallas_call(
        sums_kernel,
        out_shape=jax.ShapeDtypeStruct((tiles, size + 2 * EDGE, size), jnp.bfloat16),
        in_specs=[hbm] * 8,
        out_specs=pl.BlockSpec(memory_space=pltpu.VMEM),
        scratch_shapes=[
            pltpu.VMEM((count, size, size), jnp.bfloat16),
            pltpu.VMEM(words.shape, jnp.int32),
            pltpu.VMEM(taps.shape, jnp.float32),
            pltpu.VMEM(shifts.shape, jnp.float32),
            pltpu.VMEM((2, size // 4 + 8, wide), jnp.float32),
            pltpu.VMEM((2, size, wide), jnp.float32),
            pltpu.VMEM((7, wide, size), jnp.float32),
            pltpu.VMEM((7, wide, size), jnp.float32),
            pltpu.VMEM((wide, size), jnp.float32),
            pltpu.VMEM((tiles, size, size), jnp.float32),
            pltpu.VMEM((tiles, 2 * EDGE, size), jnp.float32),
            pltpu.VMEM((size, GROUP * size), jnp.bfloat16),
            pltpu.VMEM((GROUP, size, size), jnp.bfloat16),
            pltpu.VMEM((GROUP * size, size), jnp.bfloat16),
            pltpu.VMEM((GROUP, 8, size), jnp.float32),
            pltpu.SMEM(tile.shape, jnp.int32),
            pltpu.SMEM(visit.shape, jnp.int32),
            pltpu.SMEM(calib.shape, jnp.float32),
            pltpu.SMEM(weights.shape, jnp.int32),
            pltpu.SMEM((blocks * GROUP,), jnp.int32),
            pltpu.SMEM((blocks + 1,), jnp.int32),
            pltpu.SMEM((tiles,), jnp.int32),
            pltpu.SMEM((tiles,), jnp.int32),
            pltpu.SemaphoreType.DMA((chunks,)),
            pltpu.SemaphoreType.DMA((7,)),
        ],
        compiler_params=pltpu.CompilerParams(vmem_limit_bytes=56 * 1024 * 1024),
        name="local_sums",
    )(tile, visit, calib, weights, words, taps, shifts, pieces)


def owner_kernel(
    owners, bands, gain_ref, sums_ref, coadd_ref, det_ref,
    own, got, mine, other, gain, own_sem, send_sem, recv_sem, band_send, band_recv, gain_sem,
):
    size = coadd_ref.shape[0]
    load = pltpu.make_async_copy(gain_ref, gain, gain_sem)
    load.start()
    me = lax.axis_index("vis")
    band = lax.axis_index("band")
    keep = pltpu.make_async_copy(sums_ref.at[me], own, own_sem)
    keep.start()
    barrier = pltpu.get_barrier_semaphore()
    for o in range(1, owners):
        pl.semaphore_signal(
            barrier, inc=1, device_id={"vis": lax.rem(me + o, owners)}, device_id_type=MESH
        )
    for o in range(1, bands):
        pl.semaphore_signal(
            barrier, inc=1, device_id={"band": lax.rem(band + o, bands)}, device_id_type=MESH
        )
    pl.semaphore_wait(barrier, owners + bands - 2)
    copies = []
    for o in range(1, owners):
        to = lax.rem(me + o, owners)
        copy = pltpu.make_async_remote_copy(
            src_ref=sums_ref.at[to],
            dst_ref=got.at[o],
            send_sem=send_sem.at[o],
            recv_sem=recv_sem.at[o],
            device_id={"vis": to},
            device_id_type=MESH,
        )
        copy.start()
        copies.append(copy)
    keep.wait()
    total = own[...].astype(jnp.float32)
    for o in range(1, owners):
        copies[o - 1].wait_recv()
        total = total + got[o].astype(jnp.float32)
    num = total[0:size]
    rim = jnp.maximum(total[size:], 1.0)
    inner = jnp.broadcast_to(rim[EDGE - 1 : EDGE], (size - 2 * EDGE, size))
    den = jnp.concatenate([rim[:EDGE], inner, rim[EDGE:]], axis=0)
    coadd = num / den
    coadd_ref[...] = coadd
    load.wait()
    scaled = coadd * gain[0, 0]
    mine[...] = scaled
    swaps = []
    for o in range(1, bands):
        swap = pltpu.make_async_remote_copy(
            src_ref=mine,
            dst_ref=other.at[o],
            send_sem=band_send.at[o],
            recv_sem=band_recv.at[o],
            device_id={"band": lax.rem(band + o, bands)},
            device_id_type=MESH,
        )
        swap.start()
        swaps.append(swap)
    for o in range(1, bands):
        swaps[o - 1].wait_recv()
        scaled = scaled + other[o]
    det_ref[...] = scaled
    for copy in copies + swaps:
        copy.wait_send()


def owner_coadd(gain, sums, owners, bands):
    tiles, rows, size = sums.shape
    vmem = pl.BlockSpec(memory_space=pltpu.VMEM)
    out = jax.ShapeDtypeStruct((size, size), jnp.float32)
    return pl.pallas_call(
        functools.partial(owner_kernel, owners, bands),
        out_shape=(out, out),
        in_specs=[pl.BlockSpec(memory_space=pltpu.HBM)] * 2,
        out_specs=(vmem, vmem),
        scratch_shapes=[
            pltpu.VMEM((rows, size), jnp.bfloat16),
            pltpu.VMEM((owners, rows, size), jnp.bfloat16),
            pltpu.VMEM((size, size), jnp.float32),
            pltpu.VMEM((bands, size, size), jnp.float32),
            pltpu.SMEM((1, 1), jnp.float32),
            pltpu.SemaphoreType.DMA,
            pltpu.SemaphoreType.DMA((owners,)),
            pltpu.SemaphoreType.DMA((owners,)),
            pltpu.SemaphoreType.DMA((bands,)),
            pltpu.SemaphoreType.DMA((bands,)),
            pltpu.SemaphoreType.DMA,
        ],
        compiler_params=pltpu.CompilerParams(
            collective_id=0, has_side_effects=True, vmem_limit_bytes=56 * 1024 * 1024
        ),
        name="owner_coadd",
    )(gain, sums)


def shards(pieces, visit, tile_map, good_columns, psf_taps, shifts, calib, weights, band_gain):
    owners = lax.axis_size("vis")
    sums = local_sums(
        pieces[0], visit, tile_map[:, :, 0], good_columns[0].T, psf_taps[0].transpose(2, 1, 0),
        shifts[0].T, calib, weights, owners,
    )
    coadd, detection = owner_coadd(band_gain.reshape(1, 1), sums, owners, lax.axis_size("band"))
    return (coadd[None], detection)


def solution(mesh):
    placed = (
        P("band", ("groups", "vis"), None, None),
        P("band", ("groups", "vis")),
        P("band", ("groups", "vis"), None),
        P("band", ("groups", "vis"), None),
        P("band", ("groups", "vis"), None, None),
        P("band", ("groups", "vis"), None),
        P("band", None),
        P("band", None),
        P("band"),
    )
    return jax.shard_map(
        shards,
        mesh=mesh,
        in_specs=placed,
        out_specs=(P("band", ("groups", "vis"), None), P(("groups", "vis"), None)),
        check_vma=False,
    )
```

```python
import functools
import math

import jax
import jax.numpy as jnp
from jax import lax
from jax.experimental import pallas as pl
from jax.experimental.pallas import tpu as pltpu
from jax.sharding import PartitionSpec as P

GROUP = 8
SIDE = 3
EDGE = 16
MESH = pl.DeviceIdType.MESH


def lanczos(x):
    inside = jnp.abs(x) < 3.0
    u = jnp.where(inside, x, 0.0) * (math.pi / 3.0)
    square = u * u
    q = jnp.full_like(square, -1.0 / math.factorial(23))
    for k in range(10, -1, -1):
        q = q * square + (-1.0 if k % 2 else 1.0) / math.factorial(2 * k + 1)
    q2 = q * q
    return jnp.where(inside, q2 * (1.0 - (4.0 / 3.0) * square * q2), 0.0)


def tap_columns(padded, shift, width):
    sub = lax.broadcasted_iota(jnp.int32, (8, shift.shape[1]), 0)
    w = lanczos((sub - SIDE).astype(jnp.float32) - shift)
    w = jnp.where(sub <= 2 * SIDE, w, 0.0)
    w = w / jnp.sum(w, axis=0, keepdims=True)
    w = w.astype(jnp.bfloat16).astype(jnp.float32)
    terms = [
        w[m + SIDE : m + SIDE + 1] * padded[SIDE - m : SIDE - m + width, :]
        for m in range(-SIDE, SIDE + 1)
    ]
    down = terms[6] + terms[5] + terms[4]
    first = []
    for m in range(SIDE, -1, -1):
        down = down + terms[m]
        first.append(down)
    up = terms[0] + terms[1] + terms[2]
    last = []
    for m in range(SIDE, 2 * SIDE):
        up = up + terms[m]
        last.append(up)
    return first, last


def band_matrix(ref, p, size, masks):
    sub, keep = masks
    row = [jnp.broadcast_to(ref[v, pl.ds(p, 1), :], (8, size)) for v in range(7)]
    top = jnp.where(sub == 0, row[0], jnp.where(sub == 1, row[1], jnp.where(sub == 2, row[2], row[3])))
    end = jnp.where(sub == 7, row[4], jnp.where(sub == 6, row[5], jnp.where(sub == 5, row[6], row[3])))
    base = pltpu.roll(row[3], 0, 1, stride=1, stride_axis=0)
    top = pltpu.roll(top, 0, 1, stride=1, stride_axis=0)
    end = pltpu.roll(end, size - 8, 1, stride=1, stride_axis=0)
    tiles = size // 8
    next8 = pltpu.roll(base, 8, 1)
    head = [jnp.where(keep[0], top, 0.0), jnp.where(keep[1], next8, 0.0)]
    tail = [
        jnp.where(keep[tiles - 2], pltpu.roll(base, size - 16, 1), 0.0),
        jnp.where(keep[tiles - 1], end, 0.0),
    ]
    pair = jnp.concatenate([base, next8], axis=0).astype(jnp.bfloat16)
    parts = [jnp.concatenate(head, axis=0).astype(jnp.bfloat16)]
    for v in range(1, tiles // 2 - 1):
        parts.append(pltpu.roll(pair, 16 * v, 1))
    parts.append(jnp.concatenate(tail, axis=0).astype(jnp.bfloat16))
    return parts


def sums_kernel(
    tile_hbm, visit_hbm, calib_hbm, weights_hbm, gain_hbm, words_hbm, taps_hbm, shifts_hbm, pieces_ref,
    out_ref, gain_out,
    pbuf, words_ref, taps_ref, shifts_ref, padded, columns, left_taps, right_taps, good,
    acc, dacc, lbuf, rbuf, ibuf, cbuf,
    tile_ref, visit_ref, calib_ref, weights_ref, gain_ref, slots, blk_tile, cnt, cur, sems, small_sems,
):
    count, size, _ = pieces_ref.shape
    tiles = acc.shape[0]
    chunks = sems.shape[0]
    each = count // chunks
    smalls = [
        pltpu.make_async_copy(src, dst, small_sems.at[i])
        for i, (src, dst) in enumerate(
            (
                (tile_hbm, tile_ref), (shifts_hbm, shifts_ref), (taps_hbm, taps_ref),
                (words_hbm, words_ref), (visit_hbm, visit_ref), (calib_hbm, calib_ref),
                (weights_hbm, weights_ref), (gain_hbm, gain_ref),
            )
        )
    ]
    for copy in smalls:
        copy.start()
    copies = [
        pltpu.make_async_copy(
            pieces_ref.at[pl.ds(c * each, each)], pbuf.at[pl.ds(c * each, each)], sems.at[c]
        )
        for c in range(chunks)
    ]
    for copy in copies:
        copy.start()

    def clear_slot(i, carry):
        slots[i] = -1
        return carry

    lax.fori_loop(0, slots.shape[0], clear_slot, 0, unroll=8)

    def clear_blk(i, carry):
        blk_tile[i] = 0
        return carry

    lax.fori_loop(0, blk_tile.shape[0], clear_blk, 0, unroll=8)
    for t in range(tiles):
        cnt[t] = 0
        cur[t] = 0
        acc[t] = jnp.zeros((size, size), jnp.float32)
        dacc[t] = jnp.zeros((2 * EDGE, size), jnp.float32)
    lbuf[...] = jnp.zeros_like(lbuf)
    ibuf[...] = jnp.zeros_like(ibuf)
    cbuf[...] = jnp.zeros_like(cbuf)
    padded[...] = jnp.zeros_like(padded)
    for copy in smalls:
        copy.wait()

    gain_out[...] = jnp.full(gain_out.shape, gain_ref[0, 0])

    def place(i, used):
        t = tile_ref[0, i]
        n = cnt[t]
        inside = n & (GROUP - 1)
        fresh = inside == 0
        b = jnp.where(fresh, used, cur[t])
        cur[t] = b
        blk_tile[b + 1] = t
        slots[b * GROUP + inside] = i
        cnt[t] = n + 1
        return jnp.where(fresh, used + 1, used)

    used = jnp.int32(0)
    for i in range(count):
        used = place(i, used)

    taps_count = taps_ref.shape[0]
    reach = (taps_count - 1) // 2 + SIDE
    block = size // 4
    wide = padded.shape[2]
    place_lane = lax.broadcasted_iota(jnp.int32, (size, size), 1)
    inside = (place_lane < block - reach) | (place_lane >= size - reach)
    for d, table in ((0, left_taps), (1, right_taps)):
        taps = taps_ref[:, d, :]
        kernel = taps / jnp.sum(taps, axis=0, keepdims=True)
        kernel = kernel.astype(jnp.bfloat16).astype(jnp.float32)
        padded[d, 2 * SIDE : 2 * SIDE + taps_count, 0:count] = kernel
        shift = jnp.concatenate(
            [shifts_ref[d : d + 1, :], jnp.zeros((1, wide - count), jnp.float32)], axis=1
        )
        first, last = tap_columns(padded.at[d], shift, block)
        for v, rows in enumerate(first):
            columns[0, block * v : block * (v + 1), :] = rows
        for v, rows in enumerate(last):
            columns[1, block * v : block * (v + 1), :] = rows
        columns[1, 3 * block : size, :] = first[3]
        for h in range(2):
            for c in range(wide // size):
                part = columns[h, :, c * size : (c + 1) * size]
                turned = part.T
                for v in range(4 if h == 0 else 3):
                    x = pltpu.roll(turned, (-block * v - reach) % size, 1)
                    table[4 * h + v, c * size : (c + 1) * size, :] = jnp.where(inside, x, 0.0)
    bit = lax.broadcasted_iota(jnp.int32, (32, count), 0)
    flags = [
        (lax.shift_right_logical(jnp.broadcast_to(words_ref[k : k + 1, :], (32, count)), bit) & 1)
        for k in range(size // 32)
    ]
    columns[0, :, 0:count] = jnp.concatenate(flags, axis=0).astype(jnp.float32)
    for c in range(wide // size):
        good[c * size : (c + 1) * size, :] = columns[0, :, c * size : (c + 1) * size].T

    sub = lax.broadcasted_iota(jnp.int32, (8, size), 0)
    lane = lax.broadcasted_iota(jnp.int32, (8, size), 1)
    final = size // 8 - 1
    keep = {v: jnp.abs(lane - sub - 8 * v) <= reach for v in (0, 1, final - 1, final)}
    masks = (sub, keep)

    def piece_of(step, g):
        return jnp.maximum(slots[step * GROUP + g], 0)

    def weight_of(step, g):
        p = slots[step * GROUP + g]
        v = visit_ref[0, jnp.maximum(p, 0)]
        w = jnp.where(p >= 0, weights_ref[0, v], 0).astype(jnp.float32)
        return w, w * calib_ref[0, v]

    def build_right(step):
        for g in range(GROUP):
            p = piece_of(step, g)
            mask = jnp.broadcast_to(good[pl.ds(p, 1), :], (16, size)).astype(jnp.bfloat16)
            parts = band_matrix(right_taps, p, size, masks)
            for v, part in enumerate(parts):
                rbuf[g, 16 * v : 16 * v + 16, :] = part * mask

    def build_left(step):
        for g in range(GROUP):
            p = piece_of(step, g)
            parts = band_matrix(left_taps, p, size, masks)
            for v, part in enumerate(parts):
                lbuf[16 * v : 16 * v + 16, g * size : (g + 1) * size] = part

    for copy in copies:
        copy.wait()
    build_right(0)
    ones = jnp.ones((16, size), jnp.bfloat16)

    def step_body(k, carry):
        t = blk_tile[k]
        part = jnp.dot(lbuf[...], ibuf[...], preferred_element_type=jnp.float32)
        acc[t] = acc[t] + part
        den = dacc[t]
        for g in range(GROUP):
            cols = slice(g * size, (g + 1) * size)
            rim = jnp.concatenate(
                [lbuf[0:EDGE, cols], lbuf[size - EDGE : size, cols]], axis=0
            ).astype(jnp.float32)
            den = den + jnp.sum(rim, axis=1, keepdims=True) * cbuf[g, 0:1, :]
        dacc[t] = den
        for g in range(GROUP):
            p = piece_of(k, g)
            w, factor = weight_of(k, g)
            x = jnp.concatenate([pbuf[p], ones], axis=0)
            y = lax.dot_general(
                x, rbuf[g], (((1,), (1,)), ((), ())), preferred_element_type=jnp.float32
            )
            ibuf[g * size : (g + 1) * size, :] = (y[0:size] * factor).astype(jnp.bfloat16)
            cbuf[g] = y[size : size + 8] * w
        build_left(k)
        build_right(k + 1)
        return carry

    lax.fori_loop(0, used + 1, step_body, 0)
    for t in range(tiles):
        out_ref[t, 0:size, :] = acc[t].astype(jnp.bfloat16)
        out_ref[t, size : size + 2 * EDGE, :] = dacc[t].astype(jnp.bfloat16)


def local_sums(pieces, visit, tile, words, taps, shifts, calib, weights, gain, tiles):
    count, size, _ = pieces.shape
    blocks = (count + tiles * (GROUP - 1)) // GROUP + 2
    hbm = pl.BlockSpec(memory_space=pltpu.HBM)
    chunks = 8 if count % 8 == 0 else 1
    wide = -(-count // size) * size
    return pl.pallas_call(
        sums_kernel,
        out_shape=(
            jax.ShapeDtypeStruct((tiles, size + 2 * EDGE, size), jnp.bfloat16),
            jax.ShapeDtypeStruct((8, size), jnp.float32),
        ),
        in_specs=[hbm] * 9,
        out_specs=(pl.BlockSpec(memory_space=pltpu.VMEM),) * 2,
        scratch_shapes=[
            pltpu.VMEM((count, size, size), jnp.bfloat16),
            pltpu.VMEM(words.shape, jnp.int32),
            pltpu.VMEM(taps.shape, jnp.float32),
            pltpu.VMEM(shifts.shape, jnp.float32),
            pltpu.VMEM((2, size // 4 + 8, wide), jnp.float32),
            pltpu.VMEM((2, size, wide), jnp.float32),
            pltpu.VMEM((7, wide, size), jnp.float32),
            pltpu.VMEM((7, wide, size), jnp.float32),
            pltpu.VMEM((wide, size), jnp.float32),
            pltpu.VMEM((tiles, size, size), jnp.float32),
            pltpu.VMEM((tiles, 2 * EDGE, size), jnp.float32),
            pltpu.VMEM((size, GROUP * size), jnp.bfloat16),
            pltpu.VMEM((GROUP, size, size), jnp.bfloat16),
            pltpu.VMEM((GROUP * size, size), jnp.bfloat16),
            pltpu.VMEM((GROUP, 8, size), jnp.float32),
            pltpu.SMEM(tile.shape, jnp.int32),
            pltpu.SMEM(visit.shape, jnp.int32),
            pltpu.SMEM(calib.shape, jnp.float32),
            pltpu.SMEM(weights.shape, jnp.int32),
            pltpu.SMEM(gain.shape, jnp.float32),
            pltpu.SMEM((blocks * GROUP,), jnp.int32),
            pltpu.SMEM((blocks + 1,), jnp.int32),
            pltpu.SMEM((tiles,), jnp.int32),
            pltpu.SMEM((tiles,), jnp.int32),
            pltpu.SemaphoreType.DMA((chunks,)),
            pltpu.SemaphoreType.DMA((8,)),
        ],
        compiler_params=pltpu.CompilerParams(vmem_limit_bytes=56 * 1024 * 1024),
        name="local_sums",
    )(tile, visit, calib, weights, gain, words, taps, shifts, pieces)


def owner_kernel(
    owners, bands, gain_ref, sums_ref, coadd_ref, det_ref,
    own, near, pair, far, mine, other, gain, gain_sem, own_sem,
    near_send, near_recv, far_send, far_recv, band_send, band_recv,
):
    size = coadd_ref.shape[0]
    half = owners // 2
    me = lax.axis_index("vis")
    band = lax.axis_index("band")
    mate = me + 1 - 2 * lax.rem(me, 2)
    load = pltpu.make_async_copy(gain_ref, gain, gain_sem)
    load.start()
    order = list(range(1, half)) + [0]
    fetch = {}
    for o in order:
        fetch[o] = pltpu.make_async_copy(
            sums_ref.at[lax.rem(me + 2 * o, owners)], own.at[o], own_sem.at[o]
        )
        fetch[o].start()
    barrier = pltpu.get_barrier_semaphore()
    pl.semaphore_signal(barrier, inc=1, device_id={"vis": mate}, device_id_type=MESH)
    for o in range(1, half):
        pl.semaphore_signal(
            barrier, inc=1, device_id={"vis": lax.rem(me + 2 * o, owners)}, device_id_type=MESH
        )
    for o in range(1, bands):
        pl.semaphore_signal(
            barrier, inc=1, device_id={"band": lax.rem(band + o, bands)}, device_id_type=MESH
        )
    pl.semaphore_wait(barrier, half + bands - 1)
    nears, fars = {}, {}
    for o in order:
        nears[o] = pltpu.make_async_remote_copy(
            src_ref=sums_ref.at[lax.rem(mate + 2 * o, owners)],
            dst_ref=near.at[o],
            send_sem=near_send.at[o],
            recv_sem=near_recv.at[o],
            device_id={"vis": mate},
            device_id_type=MESH,
        )
        nears[o].start()
    total = None
    for o in order:
        fetch[o].wait()
        nears[o].wait_recv()
        both = own[o].astype(jnp.float32) + near[o].astype(jnp.float32)
        if o == 0:
            total = both
            continue
        pair[o] = both.astype(jnp.bfloat16)
        fars[o] = pltpu.make_async_remote_copy(
            src_ref=pair.at[o],
            dst_ref=far.at[o],
            send_sem=far_send.at[o],
            recv_sem=far_recv.at[o],
            device_id={"vis": lax.rem(me + 2 * o, owners)},
            device_id_type=MESH,
        )
        fars[o].start()
    for o in range(1, half):
        fars[o].wait_recv()
        total = total + far[o].astype(jnp.float32)
    num = total[0:size]
    rim = jnp.maximum(total[size:], 1.0)
    inner = jnp.broadcast_to(rim[EDGE - 1 : EDGE], (size - 2 * EDGE, size))
    den = jnp.concatenate([rim[:EDGE], inner, rim[EDGE:]], axis=0)
    coadd = num / den
    coadd_ref[...] = coadd
    load.wait()
    scaled = coadd * gain[0:1, :]
    mine[...] = scaled
    swaps = []
    for o in range(1, bands):
        swap = pltpu.make_async_remote_copy(
            src_ref=mine,
            dst_ref=other.at[o],
            send_sem=band_send.at[o],
            recv_sem=band_recv.at[o],
            device_id={"band": lax.rem(band + o, bands)},
            device_id_type=MESH,
        )
        swap.start()
        swaps.append(swap)
    for o in range(1, bands):
        swaps[o - 1].wait_recv()
        scaled = scaled + other[o]
    det_ref[...] = scaled
    for copy in list(nears.values()) + list(fars.values()) + swaps:
        copy.wait_send()


def owner_coadd(gain, sums, owners, bands):
    tiles, rows, size = sums.shape
    half = owners // 2
    vmem = pl.BlockSpec(memory_space=pltpu.VMEM)
    out = jax.ShapeDtypeStruct((size, size), jnp.float32)
    return pl.pallas_call(
        functools.partial(owner_kernel, owners, bands),
        out_shape=(out, out),
        in_specs=[pl.BlockSpec(memory_space=pltpu.HBM)] * 2,
        out_specs=(vmem, vmem),
        scratch_shapes=[
            pltpu.VMEM((half, rows, size), jnp.bfloat16),
            pltpu.VMEM((half, rows, size), jnp.bfloat16),
            pltpu.VMEM((half, rows, size), jnp.bfloat16),
            pltpu.VMEM((half, rows, size), jnp.bfloat16),
            pltpu.VMEM((size, size), jnp.float32),
            pltpu.VMEM((bands, size, size), jnp.float32),
            pltpu.VMEM(gain.shape, jnp.float32),
            pltpu.SemaphoreType.DMA,
            pltpu.SemaphoreType.DMA((half,)),
            pltpu.SemaphoreType.DMA((half,)),
            pltpu.SemaphoreType.DMA((half,)),
            pltpu.SemaphoreType.DMA((half,)),
            pltpu.SemaphoreType.DMA((half,)),
            pltpu.SemaphoreType.DMA((bands,)),
            pltpu.SemaphoreType.DMA((bands,)),
        ],
        compiler_params=pltpu.CompilerParams(
            collective_id=0, has_side_effects=True, vmem_limit_bytes=56 * 1024 * 1024
        ),
        name="owner_coadd",
    )(gain, sums)


def write_kernel(coadd_ref, det_ref, coadd_out, det_out):
    coadd_out[...] = coadd_ref[...]
    det_out[...] = det_ref[...]


def write_out(coadd, detection):
    vmem = pl.BlockSpec(memory_space=pltpu.VMEM)
    out = jax.ShapeDtypeStruct(coadd.shape, coadd.dtype)
    return pl.pallas_call(
        write_kernel,
        out_shape=(out, out),
        in_specs=[vmem, vmem],
        out_specs=(vmem, vmem),
        compiler_params=pltpu.CompilerParams(vmem_limit_bytes=56 * 1024 * 1024),
        name="write_out",
    )(coadd, detection)


def shards(pieces, visit, tile_map, good_columns, psf_taps, shifts, calib, weights, band_gain):
    owners = lax.axis_size("vis")
    sums, gain = local_sums(
        pieces[0], visit, tile_map[:, :, 0], good_columns[0].T, psf_taps[0].transpose(2, 1, 0),
        shifts[0].T, calib, weights, band_gain.reshape(1, 1), owners,
    )
    coadd, detection = owner_coadd(gain, sums, owners, lax.axis_size("band"))
    coadd, detection = write_out(coadd, detection)
    return (coadd[None], detection)


def solution(mesh):
    placed = (
        P("band", ("groups", "vis"), None, None),
        P("band", ("groups", "vis")),
        P("band", ("groups", "vis"), None),
        P("band", ("groups", "vis"), None),
        P("band", ("groups", "vis"), None, None),
        P("band", ("groups", "vis"), None),
        P("band", None),
        P("band", None),
        P("band"),
    )
    return jax.shard_map(
        shards,
        mesh=mesh,
        in_specs=placed,
        out_specs=(P("band", ("groups", "vis"), None), P(("groups", "vis"), None)),
        check_vma=False,
    )
```

```python
import functools
import math

import jax
import jax.numpy as jnp
from jax import lax
from jax.experimental import pallas as pl
from jax.experimental.pallas import tpu as pltpu
from jax.sharding import PartitionSpec as P

GROUP = 8
SIDE = 3
EDGE = 16
MESH = pl.DeviceIdType.MESH


def lanczos(x):
    inside = jnp.abs(x) < 3.0
    u = jnp.where(inside, x, 0.0) * (math.pi / 3.0)
    square = u * u
    q = jnp.full_like(square, -1.0 / math.factorial(23))
    for k in range(10, -1, -1):
        q = q * square + (-1.0 if k % 2 else 1.0) / math.factorial(2 * k + 1)
    q2 = q * q
    return jnp.where(inside, q2 * (1.0 - (4.0 / 3.0) * square * q2), 0.0)


def tap_columns(padded, shift, width):
    sub = lax.broadcasted_iota(jnp.int32, (8, shift.shape[1]), 0)
    w = lanczos((sub - SIDE).astype(jnp.float32) - shift)
    w = jnp.where(sub <= 2 * SIDE, w, 0.0)
    w = w / jnp.sum(w, axis=0, keepdims=True)
    w = w.astype(jnp.bfloat16).astype(jnp.float32)
    terms = [
        w[m + SIDE : m + SIDE + 1] * padded[SIDE - m : SIDE - m + width, :]
        for m in range(-SIDE, SIDE + 1)
    ]
    down = terms[6] + terms[5] + terms[4]
    first = []
    for m in range(SIDE, -1, -1):
        down = down + terms[m]
        first.append(down)
    up = terms[0] + terms[1] + terms[2]
    last = []
    for m in range(SIDE, 2 * SIDE):
        up = up + terms[m]
        last.append(up)
    return first, last


def spread(ref, p, size):
    return [jnp.broadcast_to(ref[v, pl.ds(p, 1), :], (8, size)) for v in range(7)]


def turn(x, shift, size):
    return pltpu.roll(x, shift % size, 1, stride=1, stride_axis=0)


def assemble(base, top, second, before, end, keep, size):
    tiles = size // 8
    head = [jnp.where(keep[0], top, 0.0), jnp.where(keep[1], second, 0.0)]
    tail = [jnp.where(keep[tiles - 2], before, 0.0), jnp.where(keep[tiles - 1], end, 0.0)]
    pair = jnp.concatenate([base, pltpu.roll(base, 8, 1)], axis=0).astype(jnp.bfloat16)
    parts = [jnp.concatenate(head, axis=0).astype(jnp.bfloat16)]
    for v in range(1, tiles // 2 - 1):
        parts.append(pltpu.roll(pair, 16 * v, 1))
    parts.append(jnp.concatenate(tail, axis=0).astype(jnp.bfloat16))
    return parts


def row_band(ref, p, size, sub, keep):
    row = spread(ref, p, size)
    top = jnp.where(sub == 0, row[0], jnp.where(sub == 1, row[1], jnp.where(sub == 2, row[2], row[3])))
    end = jnp.where(sub == 7, row[4], jnp.where(sub == 6, row[5], jnp.where(sub == 5, row[6], row[3])))
    base = turn(row[3], 0, size)
    return assemble(
        base, turn(top, 0, size), pltpu.roll(base, 8, 1), pltpu.roll(base, size - 16, 1),
        turn(end, size - 8, size), keep, size,
    )


def column_band(ref, p, size, spots, keep):
    row = spread(ref, p, size)

    def edged(tile, three):
        x = row[3]
        for i in range(3):
            x = jnp.where(spots[tile, i], row[three + i], x)
        return turn(x, 8 * tile, size)

    last = size // 8 - 1
    return assemble(
        turn(row[3], 0, size), edged(0, 0), edged(1, 0), edged(last - 1, 4), edged(last, 4),
        keep, size,
    )


def sums_kernel(
    tile_hbm, visit_hbm, calib_hbm, weights_hbm, gain_ref, words_hbm, taps_hbm, shifts_hbm, pieces_ref,
    out_ref, gain_out,
    pbuf, words_ref, taps_ref, shifts_ref, padded, columns, left_taps, right_taps, good,
    acc, dacc, lbuf, rbuf, ibuf, cbuf,
    tile_ref, visit_ref, calib_ref, weights_ref, slots, blk_tile, cnt, cur, sems, small_sems,
):
    count, size, _ = pieces_ref.shape
    tiles = acc.shape[0]
    chunks = sems.shape[0]
    each = count // chunks
    smalls = [
        pltpu.make_async_copy(src, dst, small_sems.at[i])
        for i, (src, dst) in enumerate(
            (
                (tile_hbm, tile_ref), (shifts_hbm, shifts_ref), (taps_hbm, taps_ref),
                (words_hbm, words_ref), (visit_hbm, visit_ref), (calib_hbm, calib_ref),
                (weights_hbm, weights_ref),
            )
        )
    ]
    for copy in smalls:
        copy.start()
    copies = [
        pltpu.make_async_copy(
            pieces_ref.at[pl.ds(c * each, each)], pbuf.at[pl.ds(c * each, each)], sems.at[c]
        )
        for c in range(chunks)
    ]
    for copy in copies:
        copy.start()

    def clear_slot(i, carry):
        slots[i] = -1
        return carry

    lax.fori_loop(0, slots.shape[0], clear_slot, 0, unroll=8)

    def clear_blk(i, carry):
        blk_tile[i] = 0
        return carry

    lax.fori_loop(0, blk_tile.shape[0], clear_blk, 0, unroll=8)
    for t in range(tiles):
        cnt[t] = 0
        cur[t] = 0
        acc[t] = jnp.zeros((size, size), jnp.float32)
        dacc[t] = jnp.zeros((2 * EDGE, size), jnp.float32)
    lbuf[...] = jnp.zeros_like(lbuf)
    ibuf[...] = jnp.zeros_like(ibuf)
    cbuf[...] = jnp.zeros_like(cbuf)
    padded[...] = jnp.zeros_like(padded)
    for copy in smalls:
        copy.wait()

    gain_out[...] = jnp.full(gain_out.shape, gain_ref[0])

    def place(i, used):
        t = tile_ref[0, i]
        n = cnt[t]
        inside = n & (GROUP - 1)
        fresh = inside == 0
        b = jnp.where(fresh, used, cur[t])
        cur[t] = b
        blk_tile[b + 1] = t
        slots[b * GROUP + inside] = i
        cnt[t] = n + 1
        return jnp.where(fresh, used + 1, used)

    used = jnp.int32(0)
    for i in range(count):
        used = place(i, used)

    taps_count = taps_ref.shape[0]
    reach = (taps_count - 1) // 2 + SIDE
    block = size // 4
    wide = padded.shape[2]
    place_lane = lax.broadcasted_iota(jnp.int32, (size, size), 1)
    inside = (place_lane < block - reach) | (place_lane >= size - reach)
    for d, table in ((0, left_taps), (1, right_taps)):
        taps = taps_ref[:, d, :]
        if d == 1:
            taps = jnp.concatenate(
                [taps[t : t + 1, :] for t in range(taps_count - 1, -1, -1)], axis=0
            )
        kernel = taps / jnp.sum(taps, axis=0, keepdims=True)
        kernel = kernel.astype(jnp.bfloat16).astype(jnp.float32)
        padded[d, 2 * SIDE : 2 * SIDE + taps_count, 0:count] = kernel
        shift = jnp.concatenate(
            [shifts_ref[d : d + 1, :], jnp.zeros((1, wide - count), jnp.float32)], axis=1
        )
        if d == 0:
            first, last = tap_columns(padded.at[d], shift, block)
        else:
            last, first = tap_columns(padded.at[d], -shift, block)
            first, last = first + last[3:], last[:3]
        for v, rows in enumerate(first):
            columns[0, block * v : block * (v + 1), :] = rows
        for v, rows in enumerate(last):
            columns[1, block * v : block * (v + 1), :] = rows
        columns[1, 3 * block : size, :] = first[3]
        for h in range(2):
            for c in range(wide // size):
                part = columns[h, :, c * size : (c + 1) * size]
                turned = part.T
                for v in range(4 if h == 0 else 3):
                    x = pltpu.roll(turned, (-block * v - reach) % size, 1)
                    table[4 * h + v, c * size : (c + 1) * size, :] = jnp.where(inside, x, 0.0)
    bit = lax.broadcasted_iota(jnp.int32, (32, count), 0)
    flags = [
        (lax.shift_right_logical(jnp.broadcast_to(words_ref[k : k + 1, :], (32, count)), bit) & 1)
        for k in range(size // 32)
    ]
    columns[0, :, 0:count] = jnp.concatenate(flags, axis=0).astype(jnp.float32)
    for c in range(wide // size):
        good[c * size : (c + 1) * size, :] = columns[0, :, c * size : (c + 1) * size].T

    sub = lax.broadcasted_iota(jnp.int32, (8, size), 0)
    lane = lax.broadcasted_iota(jnp.int32, (8, size), 1)
    final = size // 8 - 1
    keep = {v: jnp.abs(lane - sub - 8 * v) <= reach for v in (0, 1, final - 1, final)}
    spots = {}
    for tile in (0, 1):
        for i in range(3):
            spots[tile, i] = lane == ((i - sub - 8 * tile) & (size - 1))
    for tile in (final - 1, final):
        for i in range(3):
            spots[tile, i] = lane == ((size - 1 - i - sub - 8 * tile) & (size - 1))

    def piece_of(step, g):
        return jnp.maximum(slots[step * GROUP + g], 0)

    def weight_of(step, g):
        p = slots[step * GROUP + g]
        v = visit_ref[0, jnp.maximum(p, 0)]
        w = jnp.where(p >= 0, weights_ref[0, v], 0).astype(jnp.float32)
        return w, w * calib_ref[0, v]

    def build_right(step):
        for g in range(GROUP):
            parts = column_band(right_taps, piece_of(step, g), size, spots, keep)
            for v, part in enumerate(parts):
                rbuf[g, 16 * v : 16 * v + 16, :] = part

    def build_left(step):
        for g in range(GROUP):
            parts = row_band(left_taps, piece_of(step, g), size, sub, keep)
            for v, part in enumerate(parts):
                lbuf[16 * v : 16 * v + 16, g * size : (g + 1) * size] = part

    for copy in copies:
        copy.wait()
    build_right(0)

    def add_up(k):
        t = blk_tile[k]
        part = jnp.dot(lbuf[...], ibuf[...], preferred_element_type=jnp.float32)
        acc[t] = acc[t] + part
        den = dacc[t]
        for g in range(GROUP):
            cols = slice(g * size, (g + 1) * size)
            rim = jnp.concatenate(
                [lbuf[0:EDGE, cols], lbuf[size - EDGE : size, cols]], axis=0
            ).astype(jnp.float32)
            den = den + jnp.sum(rim, axis=1, keepdims=True) * cbuf[g, 0:1, :]
        dacc[t] = den

    def step_body(k, carry):
        add_up(k)
        for g in range(GROUP):
            p = piece_of(k, g)
            w, factor = weight_of(k, g)
            mask = jnp.broadcast_to(good[pl.ds(p, 1), :], (16, size)).astype(jnp.bfloat16)
            rows = [pbuf[p, 16 * v : 16 * v + 16, :] * mask for v in range(size // 16)]
            x = jnp.concatenate(rows + [mask], axis=0)
            y = jnp.dot(x, rbuf[g], preferred_element_type=jnp.float32)
            ibuf[g * size : (g + 1) * size, :] = (y[0:size] * factor).astype(jnp.bfloat16)
            cbuf[g] = y[size : size + 8] * w
        build_left(k)
        build_right(k + 1)
        return carry

    lax.fori_loop(0, used, step_body, 0)
    add_up(used)
    for t in range(tiles):
        out_ref[t, 0:size, :] = acc[t].astype(jnp.bfloat16)
        out_ref[t, size : size + 2 * EDGE, :] = dacc[t].astype(jnp.bfloat16)


def local_sums(pieces, visit, tile, words, taps, shifts, calib, weights, gain, tiles):
    count, size, _ = pieces.shape
    blocks = (count + tiles * (GROUP - 1)) // GROUP + 2
    hbm = pl.BlockSpec(memory_space=pltpu.HBM)
    chunks = 8 if count % 8 == 0 else 1
    wide = -(-count // size) * size
    return pl.pallas_call(
        sums_kernel,
        out_shape=(
            jax.ShapeDtypeStruct((tiles, size + 2 * EDGE, size), jnp.bfloat16),
            jax.ShapeDtypeStruct((8, size), jnp.float32),
        ),
        in_specs=[hbm] * 4 + [pl.BlockSpec(memory_space=pltpu.SMEM)] + [hbm] * 4,
        out_specs=(pl.BlockSpec(memory_space=pltpu.VMEM),) * 2,
        scratch_shapes=[
            pltpu.VMEM((count, size, size), jnp.bfloat16),
            pltpu.VMEM(words.shape, jnp.int32),
            pltpu.VMEM(taps.shape, jnp.float32),
            pltpu.VMEM(shifts.shape, jnp.float32),
            pltpu.VMEM((2, size // 4 + 8, wide), jnp.float32),
            pltpu.VMEM((2, size, wide), jnp.float32),
            pltpu.VMEM((7, wide, size), jnp.float32),
            pltpu.VMEM((7, wide, size), jnp.float32),
            pltpu.VMEM((wide, size), jnp.float32),
            pltpu.VMEM((tiles, size, size), jnp.float32),
            pltpu.VMEM((tiles, 2 * EDGE, size), jnp.float32),
            pltpu.VMEM((size, GROUP * size), jnp.bfloat16),
            pltpu.VMEM((GROUP, size, size), jnp.bfloat16),
            pltpu.VMEM((GROUP * size, size), jnp.bfloat16),
            pltpu.VMEM((GROUP, 8, size), jnp.float32),
            pltpu.SMEM(tile.shape, jnp.int32),
            pltpu.SMEM(visit.shape, jnp.int32),
            pltpu.SMEM(calib.shape, jnp.float32),
            pltpu.SMEM(weights.shape, jnp.int32),
            pltpu.SMEM((blocks * GROUP,), jnp.int32),
            pltpu.SMEM((blocks + 1,), jnp.int32),
            pltpu.SMEM((tiles,), jnp.int32),
            pltpu.SMEM((tiles,), jnp.int32),
            pltpu.SemaphoreType.DMA((chunks,)),
            pltpu.SemaphoreType.DMA((7,)),
        ],
        compiler_params=pltpu.CompilerParams(vmem_limit_bytes=56 * 1024 * 1024),
        name="local_sums",
    )(tile, visit, calib, weights, gain, words, taps, shifts, pieces)


def owner_kernel(
    owners, bands, gain_ref, sums_ref, coadd_ref, det_ref,
    own, near, pair, far, mine, other, gain, gain_sem, own_sem,
    near_send, near_recv, far_send, far_recv, band_send, band_recv,
):
    size = coadd_ref.shape[0]
    half = owners // 2
    me = lax.axis_index("vis")
    band = lax.axis_index("band")
    mate = me + 1 - 2 * lax.rem(me, 2)
    load = pltpu.make_async_copy(gain_ref, gain, gain_sem)
    load.start()
    order = list(range(1, half)) + [0]
    fetch = {}
    for o in order:
        fetch[o] = pltpu.make_async_copy(
            sums_ref.at[lax.rem(me + 2 * o, owners)], own.at[o], own_sem.at[o]
        )
        fetch[o].start()
    barrier = pltpu.get_barrier_semaphore()
    pl.semaphore_signal(barrier, inc=1, device_id={"vis": mate}, device_id_type=MESH)
    for o in range(1, half):
        pl.semaphore_signal(
            barrier, inc=1, device_id={"vis": lax.rem(me + 2 * o, owners)}, device_id_type=MESH
        )
    for o in range(1, bands):
        pl.semaphore_signal(
            barrier, inc=1, device_id={"band": lax.rem(band + o, bands)}, device_id_type=MESH
        )
    pl.semaphore_wait(barrier, half + bands - 1)
    nears, fars = {}, {}
    for o in order:
        nears[o] = pltpu.make_async_remote_copy(
            src_ref=sums_ref.at[lax.rem(mate + 2 * o, owners)],
            dst_ref=near.at[o],
            send_sem=near_send.at[o],
            recv_sem=near_recv.at[o],
            device_id={"vis": mate},
            device_id_type=MESH,
        )
        nears[o].start()
    total = None
    for o in order:
        fetch[o].wait()
        nears[o].wait_recv()
        both = own[o].astype(jnp.float32) + near[o].astype(jnp.float32)
        if o == 0:
            total = both
            continue
        pair[o] = both.astype(jnp.bfloat16)
        fars[o] = pltpu.make_async_remote_copy(
            src_ref=pair.at[o],
            dst_ref=far.at[o],
            send_sem=far_send.at[o],
            recv_sem=far_recv.at[o],
            device_id={"vis": lax.rem(me + 2 * o, owners)},
            device_id_type=MESH,
        )
        fars[o].start()
    for o in range(1, half):
        fars[o].wait_recv()
        total = total + far[o].astype(jnp.float32)
    num = total[0:size]
    rim = jnp.maximum(total[size:], 1.0)
    inner = jnp.broadcast_to(rim[EDGE - 1 : EDGE], (size - 2 * EDGE, size))
    den = jnp.concatenate([rim[:EDGE], inner, rim[EDGE:]], axis=0)
    coadd = num / den
    coadd_ref[...] = coadd
    load.wait()
    scaled = coadd * gain[0:1, :]
    mine[...] = scaled
    swaps = []
    for o in range(1, bands):
        swap = pltpu.make_async_remote_copy(
            src_ref=mine,
            dst_ref=other.at[o],
            send_sem=band_send.at[o],
            recv_sem=band_recv.at[o],
            device_id={"band": lax.rem(band + o, bands)},
            device_id_type=MESH,
        )
        swap.start()
        swaps.append(swap)
    for o in range(1, bands):
        swaps[o - 1].wait_recv()
        scaled = scaled + other[o]
    det_ref[...] = scaled
    for copy in list(nears.values()) + list(fars.values()) + swaps:
        copy.wait_send()


def owner_coadd(gain, sums, owners, bands):
    tiles, rows, size = sums.shape
    half = owners // 2
    vmem = pl.BlockSpec(memory_space=pltpu.VMEM)
    out = jax.ShapeDtypeStruct((size, size), jnp.float32)
    return pl.pallas_call(
        functools.partial(owner_kernel, owners, bands),
        out_shape=(out, out),
        in_specs=[pl.BlockSpec(memory_space=pltpu.HBM)] * 2,
        out_specs=(vmem, vmem),
        scratch_shapes=[
            pltpu.VMEM((half, rows, size), jnp.bfloat16),
            pltpu.VMEM((half, rows, size), jnp.bfloat16),
            pltpu.VMEM((half, rows, size), jnp.bfloat16),
            pltpu.VMEM((half, rows, size), jnp.bfloat16),
            pltpu.VMEM((size, size), jnp.float32),
            pltpu.VMEM((bands, size, size), jnp.float32),
            pltpu.VMEM(gain.shape, jnp.float32),
            pltpu.SemaphoreType.DMA,
            pltpu.SemaphoreType.DMA((half,)),
            pltpu.SemaphoreType.DMA((half,)),
            pltpu.SemaphoreType.DMA((half,)),
            pltpu.SemaphoreType.DMA((half,)),
            pltpu.SemaphoreType.DMA((half,)),
            pltpu.SemaphoreType.DMA((bands,)),
            pltpu.SemaphoreType.DMA((bands,)),
        ],
        compiler_params=pltpu.CompilerParams(
            collective_id=0, has_side_effects=True, vmem_limit_bytes=56 * 1024 * 1024
        ),
        name="owner_coadd",
    )(gain, sums)


def write_kernel(coadd_ref, det_ref, coadd_out, det_out, sems):
    copies = [
        pltpu.make_async_copy(coadd_ref, coadd_out, sems.at[0]),
        pltpu.make_async_copy(det_ref, det_out, sems.at[1]),
    ]
    for copy in copies:
        copy.start()
    for copy in copies:
        copy.wait()


def write_out(coadd, detection):
    hbm = pl.BlockSpec(memory_space=pltpu.HBM)
    out = jax.ShapeDtypeStruct(coadd.shape, coadd.dtype)
    return pl.pallas_call(
        write_kernel,
        out_shape=(out, out),
        in_specs=[hbm, hbm],
        out_specs=(hbm, hbm),
        scratch_shapes=[pltpu.SemaphoreType.DMA((2,))],
        compiler_params=pltpu.CompilerParams(vmem_limit_bytes=56 * 1024 * 1024),
        name="write_out",
    )(coadd, detection)


def shards(pieces, visit, tile_map, good_columns, psf_taps, shifts, calib, weights, band_gain):
    owners = lax.axis_size("vis")
    sums, gain = local_sums(
        pieces[0], visit, tile_map[:, :, 0], good_columns[0].T, psf_taps[0].transpose(2, 1, 0),
        shifts[0].T, calib, weights, band_gain, owners,
    )
    coadd, detection = owner_coadd(gain, sums, owners, lax.axis_size("band"))
    coadd, detection = write_out(coadd, detection)
    return (coadd[None], detection)


def solution(mesh):
    placed = (
        P("band", ("groups", "vis"), None, None),
        P("band", ("groups", "vis")),
        P("band", ("groups", "vis"), None),
        P("band", ("groups", "vis"), None),
        P("band", ("groups", "vis"), None, None),
        P("band", ("groups", "vis"), None),
        P("band", None),
        P("band", None),
        P("band"),
    )
    return jax.shard_map(
        shards,
        mesh=mesh,
        in_specs=placed,
        out_specs=(P("band", ("groups", "vis"), None), P(("groups", "vis"), None)),
        check_vma=False,
    )
```

```python
import functools
import math

import jax
import jax.numpy as jnp
from jax import lax
from jax.experimental import pallas as pl
from jax.experimental.pallas import tpu as pltpu
from jax.sharding import PartitionSpec as P

GROUP = 8
SIDE = 3
EDGE = 16
MESH = pl.DeviceIdType.MESH


def lanczos(x):
    inside = jnp.abs(x) < 3.0
    u = jnp.where(inside, x, 0.0) * (math.pi / 3.0)
    square = u * u
    q = jnp.full_like(square, -1.0 / math.factorial(23))
    for k in range(10, -1, -1):
        q = q * square + (-1.0 if k % 2 else 1.0) / math.factorial(2 * k + 1)
    q2 = q * q
    return jnp.where(inside, q2 * (1.0 - (4.0 / 3.0) * square * q2), 0.0)


def tap_columns(padded, shift, width):
    sub = lax.broadcasted_iota(jnp.int32, (8, shift.shape[1]), 0)
    w = lanczos((sub - SIDE).astype(jnp.float32) - shift)
    w = jnp.where(sub <= 2 * SIDE, w, 0.0)
    w = w / jnp.sum(w, axis=0, keepdims=True)
    w = w.astype(jnp.bfloat16).astype(jnp.float32)
    terms = [
        w[m + SIDE : m + SIDE + 1] * padded[SIDE - m : SIDE - m + width, :]
        for m in range(-SIDE, SIDE + 1)
    ]
    down = terms[6] + terms[5] + terms[4]
    first = []
    for m in range(SIDE, -1, -1):
        down = down + terms[m]
        first.append(down)
    up = terms[0] + terms[1] + terms[2]
    last = []
    for m in range(SIDE, 2 * SIDE):
        up = up + terms[m]
        last.append(up)
    return first, last


def spread(ref, p, size):
    return [jnp.broadcast_to(ref[v, pl.ds(p, 1), :], (8, size)) for v in range(7)]


def turn(x, shift, size):
    return pltpu.roll(x, shift % size, 1, stride=1, stride_axis=0)


def assemble(base, top, second, before, end, keep, size):
    tiles = size // 8
    head = [jnp.where(keep[0], top, 0.0), jnp.where(keep[1], second, 0.0)]
    tail = [jnp.where(keep[tiles - 2], before, 0.0), jnp.where(keep[tiles - 1], end, 0.0)]
    pair = jnp.concatenate([base, pltpu.roll(base, 8, 1)], axis=0).astype(jnp.bfloat16)
    parts = [jnp.concatenate(head, axis=0).astype(jnp.bfloat16)]
    for v in range(1, tiles // 2 - 1):
        parts.append(pltpu.roll(pair, 16 * v, 1))
    parts.append(jnp.concatenate(tail, axis=0).astype(jnp.bfloat16))
    return parts


def row_band(ref, p, size, sub, keep):
    row = spread(ref, p, size)
    top = jnp.where(sub == 0, row[0], jnp.where(sub == 1, row[1], jnp.where(sub == 2, row[2], row[3])))
    end = jnp.where(sub == 7, row[4], jnp.where(sub == 6, row[5], jnp.where(sub == 5, row[6], row[3])))
    base = turn(row[3], 0, size)
    return assemble(
        base, turn(top, 0, size), pltpu.roll(base, 8, 1), pltpu.roll(base, size - 16, 1),
        turn(end, size - 8, size), keep, size,
    )


def column_band(ref, p, size, spots, keep):
    row = spread(ref, p, size)

    def edged(tile, three):
        x = row[3]
        for i in range(3):
            x = jnp.where(spots[tile, i], row[three + i], x)
        return turn(x, 8 * tile, size)

    last = size // 8 - 1
    return assemble(
        turn(row[3], 0, size), edged(0, 0), edged(1, 0), edged(last - 1, 4), edged(last, 4),
        keep, size,
    )


def sums_kernel(
    tile_hbm, visit_hbm, calib_hbm, weights_hbm, gain_ref, words_hbm, taps_hbm, shifts_hbm, pieces_ref,
    out_ref, gain_out,
    pbuf, words_ref, taps_ref, shifts_ref, padded, columns, left_taps, right_taps, good,
    acc, dacc, lbuf, rbuf, ibuf, cbuf,
    tile_ref, visit_ref, calib_ref, weights_ref, slots, blk_tile, cnt, cur, sems, small_sems,
):
    count, size, _ = pieces_ref.shape
    tiles = acc.shape[0]
    chunks = sems.shape[0]
    each = count // chunks
    smalls = [
        pltpu.make_async_copy(src, dst, small_sems.at[i])
        for i, (src, dst) in enumerate(
            (
                (tile_hbm, tile_ref), (shifts_hbm, shifts_ref), (taps_hbm, taps_ref),
                (words_hbm, words_ref), (visit_hbm, visit_ref), (calib_hbm, calib_ref),
                (weights_hbm, weights_ref),
            )
        )
    ]
    for copy in smalls:
        copy.start()
    copies = [
        pltpu.make_async_copy(
            pieces_ref.at[pl.ds(c * each, each)], pbuf.at[pl.ds(c * each, each)], sems.at[c]
        )
        for c in range(chunks)
    ]
    for copy in copies:
        copy.start()

    def clear_slot(i, carry):
        slots[i] = -1
        return carry

    lax.fori_loop(0, slots.shape[0], clear_slot, 0, unroll=8)

    def clear_blk(i, carry):
        blk_tile[i] = 0
        return carry

    lax.fori_loop(0, blk_tile.shape[0], clear_blk, 0, unroll=8)
    for t in range(tiles):
        cnt[t] = 0
        cur[t] = 0
        acc[t] = jnp.zeros((size, size), jnp.float32)
        dacc[t] = jnp.zeros((2 * EDGE, size), jnp.float32)
    lbuf[...] = jnp.zeros_like(lbuf)
    ibuf[...] = jnp.zeros_like(ibuf)
    cbuf[...] = jnp.zeros_like(cbuf)
    padded[...] = jnp.zeros_like(padded)
    for copy in smalls:
        copy.wait()

    gain_out[...] = jnp.full(gain_out.shape, gain_ref[0])

    def place(i, used):
        t = tile_ref[0, i]
        n = cnt[t]
        inside = n & (GROUP - 1)
        fresh = inside == 0
        b = jnp.where(fresh, used, cur[t])
        cur[t] = b
        blk_tile[b + 1] = t
        slots[b * GROUP + inside] = i
        cnt[t] = n + 1
        return jnp.where(fresh, used + 1, used)

    used = jnp.int32(0)
    for i in range(count):
        used = place(i, used)

    taps_count = taps_ref.shape[0]
    reach = (taps_count - 1) // 2 + SIDE
    block = size // 4
    wide = padded.shape[2]
    place_lane = lax.broadcasted_iota(jnp.int32, (size, size), 1)
    inside = (place_lane < block - reach) | (place_lane >= size - reach)
    for d, table in ((0, left_taps), (1, right_taps)):
        taps = taps_ref[:, d, :]
        if d == 1:
            taps = jnp.concatenate(
                [taps[t : t + 1, :] for t in range(taps_count - 1, -1, -1)], axis=0
            )
        kernel = taps / jnp.sum(taps, axis=0, keepdims=True)
        kernel = kernel.astype(jnp.bfloat16).astype(jnp.float32)
        padded[d, 2 * SIDE : 2 * SIDE + taps_count, 0:count] = kernel
        shift = jnp.concatenate(
            [shifts_ref[d : d + 1, :], jnp.zeros((1, wide - count), jnp.float32)], axis=1
        )
        if d == 0:
            first, last = tap_columns(padded.at[d], shift, block)
        else:
            last, first = tap_columns(padded.at[d], -shift, block)
            first, last = first + last[3:], last[:3]
        for v, rows in enumerate(first):
            columns[0, block * v : block * (v + 1), :] = rows
        for v, rows in enumerate(last):
            columns[1, block * v : block * (v + 1), :] = rows
        columns[1, 3 * block : size, :] = first[3]
        for h in range(2):
            for c in range(wide // size):
                part = columns[h, :, c * size : (c + 1) * size]
                turned = part.T
                for v in range(4 if h == 0 else 3):
                    x = pltpu.roll(turned, (-block * v - reach) % size, 1)
                    table[4 * h + v, c * size : (c + 1) * size, :] = jnp.where(inside, x, 0.0)
    bit = lax.broadcasted_iota(jnp.int32, (32, count), 0)
    flags = [
        (lax.shift_right_logical(jnp.broadcast_to(words_ref[k : k + 1, :], (32, count)), bit) & 1)
        for k in range(size // 32)
    ]
    columns[0, :, 0:count] = jnp.concatenate(flags, axis=0).astype(jnp.float32)
    for c in range(wide // size):
        good[c * size : (c + 1) * size, :] = columns[0, :, c * size : (c + 1) * size].T

    sub = lax.broadcasted_iota(jnp.int32, (8, size), 0)
    lane = lax.broadcasted_iota(jnp.int32, (8, size), 1)
    final = size // 8 - 1
    keep = {v: jnp.abs(lane - sub - 8 * v) <= reach for v in (0, 1, final - 1, final)}
    spots = {}
    for tile in (0, 1):
        for i in range(3):
            spots[tile, i] = lane == ((i - sub - 8 * tile) & (size - 1))
    for tile in (final - 1, final):
        for i in range(3):
            spots[tile, i] = lane == ((size - 1 - i - sub - 8 * tile) & (size - 1))

    def piece_of(step, g):
        return jnp.maximum(slots[step * GROUP + g], 0)

    def weight_of(step, g):
        p = slots[step * GROUP + g]
        v = visit_ref[0, jnp.maximum(p, 0)]
        w = jnp.where(p >= 0, weights_ref[0, v], 0).astype(jnp.float32)
        return w, w * calib_ref[0, v]

    def build_right(step, g):
        parts = column_band(right_taps, piece_of(step, g), size, spots, keep)
        for v, part in enumerate(parts):
            rbuf[g, 16 * v : 16 * v + 16, :] = part

    def build_left(step, g):
        parts = row_band(left_taps, piece_of(step, g), size, sub, keep)
        for v, part in enumerate(parts):
            lbuf[16 * v : 16 * v + 16, g * size : (g + 1) * size] = part

    for g in range(GROUP):
        build_right(0, g)
    for copy in copies:
        copy.wait()

    def add_up(k):
        t = blk_tile[k]
        part = jnp.dot(lbuf[...], ibuf[...], preferred_element_type=jnp.float32)
        acc[t] = acc[t] + part
        den = dacc[t]
        for g in range(GROUP):
            cols = slice(g * size, (g + 1) * size)
            rim = jnp.concatenate(
                [lbuf[0:EDGE, cols], lbuf[size - EDGE : size, cols]], axis=0
            ).astype(jnp.float32)
            den = den + jnp.sum(rim, axis=1, keepdims=True) * cbuf[g, 0:1, :]
        dacc[t] = den

    def step_body(k, carry):
        add_up(k)
        for g in range(GROUP):
            p = piece_of(k, g)
            w, factor = weight_of(k, g)
            mask = jnp.broadcast_to(good[pl.ds(p, 1), :], (16, size)).astype(jnp.bfloat16)
            rows = [pbuf[p, 16 * v : 16 * v + 16, :] * mask for v in range(size // 16)]
            x = jnp.concatenate(rows + [mask], axis=0)
            y = jnp.dot(x, rbuf[g], preferred_element_type=jnp.float32)
            ibuf[g * size : (g + 1) * size, :] = (y[0:size] * factor).astype(jnp.bfloat16)
            cbuf[g] = y[size : size + 8] * w
            build_left(k, g)
            build_right(k + 1, g)
        return carry

    lax.fori_loop(0, used, step_body, 0)
    add_up(used)
    for t in range(tiles):
        out_ref[t, 0:size, :] = acc[t].astype(jnp.bfloat16)
        out_ref[t, size : size + 2 * EDGE, :] = dacc[t].astype(jnp.bfloat16)


def local_sums(pieces, visit, tile, words, taps, shifts, calib, weights, gain, tiles):
    count, size, _ = pieces.shape
    blocks = (count + tiles * (GROUP - 1)) // GROUP + 2
    hbm = pl.BlockSpec(memory_space=pltpu.HBM)
    chunks = 8 if count % 8 == 0 else 1
    wide = -(-count // size) * size
    return pl.pallas_call(
        sums_kernel,
        out_shape=(
            jax.ShapeDtypeStruct((tiles, size + 2 * EDGE, size), jnp.bfloat16),
            jax.ShapeDtypeStruct((8, size), jnp.float32),
        ),
        in_specs=[hbm] * 4 + [pl.BlockSpec(memory_space=pltpu.SMEM)] + [hbm] * 4,
        out_specs=(pl.BlockSpec(memory_space=pltpu.VMEM),) * 2,
        scratch_shapes=[
            pltpu.VMEM((count, size, size), jnp.bfloat16),
            pltpu.VMEM(words.shape, jnp.int32),
            pltpu.VMEM(taps.shape, jnp.float32),
            pltpu.VMEM(shifts.shape, jnp.float32),
            pltpu.VMEM((2, size // 4 + 8, wide), jnp.float32),
            pltpu.VMEM((2, size, wide), jnp.float32),
            pltpu.VMEM((7, wide, size), jnp.float32),
            pltpu.VMEM((7, wide, size), jnp.float32),
            pltpu.VMEM((wide, size), jnp.float32),
            pltpu.VMEM((tiles, size, size), jnp.float32),
            pltpu.VMEM((tiles, 2 * EDGE, size), jnp.float32),
            pltpu.VMEM((size, GROUP * size), jnp.bfloat16),
            pltpu.VMEM((GROUP, size, size), jnp.bfloat16),
            pltpu.VMEM((GROUP * size, size), jnp.bfloat16),
            pltpu.VMEM((GROUP, 8, size), jnp.float32),
            pltpu.SMEM(tile.shape, jnp.int32),
            pltpu.SMEM(visit.shape, jnp.int32),
            pltpu.SMEM(calib.shape, jnp.float32),
            pltpu.SMEM(weights.shape, jnp.int32),
            pltpu.SMEM((blocks * GROUP,), jnp.int32),
            pltpu.SMEM((blocks + 1,), jnp.int32),
            pltpu.SMEM((tiles,), jnp.int32),
            pltpu.SMEM((tiles,), jnp.int32),
            pltpu.SemaphoreType.DMA((chunks,)),
            pltpu.SemaphoreType.DMA((7,)),
        ],
        compiler_params=pltpu.CompilerParams(vmem_limit_bytes=56 * 1024 * 1024),
        name="local_sums",
    )(tile, visit, calib, weights, gain, words, taps, shifts, pieces)


def owner_kernel(
    owners, bands, gain_ref, sums_ref, coadd_ref, det_ref,
    own, near, pair, far, mine, other, gain, gain_sem, own_sem,
    near_send, near_recv, far_send, far_recv, band_send, band_recv,
):
    size = coadd_ref.shape[0]
    half = owners // 2
    me = lax.axis_index("vis")
    band = lax.axis_index("band")
    mate = me + 1 - 2 * lax.rem(me, 2)
    load = pltpu.make_async_copy(gain_ref, gain, gain_sem)
    load.start()
    order = list(range(1, half)) + [0]
    fetch = {}
    for o in order:
        fetch[o] = pltpu.make_async_copy(
            sums_ref.at[lax.rem(me + 2 * o, owners)], own.at[o], own_sem.at[o]
        )
        fetch[o].start()
    barrier = pltpu.get_barrier_semaphore()
    pl.semaphore_signal(barrier, inc=1, device_id={"vis": mate}, device_id_type=MESH)
    for o in range(1, half):
        pl.semaphore_signal(
            barrier, inc=1, device_id={"vis": lax.rem(me + 2 * o, owners)}, device_id_type=MESH
        )
    for o in range(1, bands):
        pl.semaphore_signal(
            barrier, inc=1, device_id={"band": lax.rem(band + o, bands)}, device_id_type=MESH
        )
    pl.semaphore_wait(barrier, half + bands - 1)
    nears, fars = {}, {}
    for o in order:
        nears[o] = pltpu.make_async_remote_copy(
            src_ref=sums_ref.at[lax.rem(mate + 2 * o, owners)],
            dst_ref=near.at[o],
            send_sem=near_send.at[o],
            recv_sem=near_recv.at[o],
            device_id={"vis": mate},
            device_id_type=MESH,
        )
        nears[o].start()
    total = None
    for o in order:
        fetch[o].wait()
        nears[o].wait_recv()
        both = own[o].astype(jnp.float32) + near[o].astype(jnp.float32)
        if o == 0:
            total = both
            continue
        pair[o] = both.astype(jnp.bfloat16)
        fars[o] = pltpu.make_async_remote_copy(
            src_ref=pair.at[o],
            dst_ref=far.at[o],
            send_sem=far_send.at[o],
            recv_sem=far_recv.at[o],
            device_id={"vis": lax.rem(me + 2 * o, owners)},
            device_id_type=MESH,
        )
        fars[o].start()
    for o in range(1, half):
        fars[o].wait_recv()
        total = total + far[o].astype(jnp.float32)
    num = total[0:size]
    rim = jnp.maximum(total[size:], 1.0)
    inner = jnp.broadcast_to(rim[EDGE - 1 : EDGE], (size - 2 * EDGE, size))
    den = jnp.concatenate([rim[:EDGE], inner, rim[EDGE:]], axis=0)
    coadd = num / den
    coadd_ref[...] = coadd
    load.wait()
    scaled = coadd * gain[0:1, :]
    mine[...] = scaled
    swaps = []
    for o in range(1, bands):
        swap = pltpu.make_async_remote_copy(
            src_ref=mine,
            dst_ref=other.at[o],
            send_sem=band_send.at[o],
            recv_sem=band_recv.at[o],
            device_id={"band": lax.rem(band + o, bands)},
            device_id_type=MESH,
        )
        swap.start()
        swaps.append(swap)
    for o in range(1, bands):
        swaps[o - 1].wait_recv()
        scaled = scaled + other[o]
    det_ref[...] = scaled
    for copy in list(nears.values()) + list(fars.values()) + swaps:
        copy.wait_send()


def owner_coadd(gain, sums, owners, bands):
    tiles, rows, size = sums.shape
    half = owners // 2
    vmem = pl.BlockSpec(memory_space=pltpu.VMEM)
    out = jax.ShapeDtypeStruct((size, size), jnp.float32)
    return pl.pallas_call(
        functools.partial(owner_kernel, owners, bands),
        out_shape=(out, out),
        in_specs=[pl.BlockSpec(memory_space=pltpu.HBM)] * 2,
        out_specs=(vmem, vmem),
        scratch_shapes=[
            pltpu.VMEM((half, rows, size), jnp.bfloat16),
            pltpu.VMEM((half, rows, size), jnp.bfloat16),
            pltpu.VMEM((half, rows, size), jnp.bfloat16),
            pltpu.VMEM((half, rows, size), jnp.bfloat16),
            pltpu.VMEM((size, size), jnp.float32),
            pltpu.VMEM((bands, size, size), jnp.float32),
            pltpu.VMEM(gain.shape, jnp.float32),
            pltpu.SemaphoreType.DMA,
            pltpu.SemaphoreType.DMA((half,)),
            pltpu.SemaphoreType.DMA((half,)),
            pltpu.SemaphoreType.DMA((half,)),
            pltpu.SemaphoreType.DMA((half,)),
            pltpu.SemaphoreType.DMA((half,)),
            pltpu.SemaphoreType.DMA((bands,)),
            pltpu.SemaphoreType.DMA((bands,)),
        ],
        compiler_params=pltpu.CompilerParams(
            collective_id=0, has_side_effects=True, vmem_limit_bytes=56 * 1024 * 1024
        ),
        name="owner_coadd",
    )(gain, sums)


def write_kernel(coadd_ref, det_ref, coadd_out, det_out):
    coadd_out[...] = coadd_ref[...]
    det_out[...] = det_ref[...]


def write_out(coadd, detection):
    vmem = pl.BlockSpec(memory_space=pltpu.VMEM)
    out = jax.ShapeDtypeStruct(coadd.shape, coadd.dtype)
    return pl.pallas_call(
        write_kernel,
        out_shape=(out, out),
        in_specs=[vmem, vmem],
        out_specs=(vmem, vmem),
        compiler_params=pltpu.CompilerParams(vmem_limit_bytes=56 * 1024 * 1024),
        name="write_out",
    )(coadd, detection)


def shards(pieces, visit, tile_map, good_columns, psf_taps, shifts, calib, weights, band_gain):
    owners = lax.axis_size("vis")
    sums, gain = local_sums(
        pieces[0], visit, tile_map[:, :, 0], good_columns[0].T, psf_taps[0].transpose(2, 1, 0),
        shifts[0].T, calib, weights, band_gain, owners,
    )
    coadd, detection = owner_coadd(gain, sums, owners, lax.axis_size("band"))
    coadd, detection = write_out(coadd, detection)
    return (coadd[None], detection)


def solution(mesh):
    placed = (
        P("band", ("groups", "vis"), None, None),
        P("band", ("groups", "vis")),
        P("band", ("groups", "vis"), None),
        P("band", ("groups", "vis"), None),
        P("band", ("groups", "vis"), None, None),
        P("band", ("groups", "vis"), None),
        P("band", None),
        P("band", None),
        P("band"),
    )
    return jax.shard_map(
        shards,
        mesh=mesh,
        in_specs=placed,
        out_specs=(P("band", ("groups", "vis"), None), P(("groups", "vis"), None)),
        check_vma=False,
    )
```

```python
import functools
import math

import jax
import jax.numpy as jnp
from jax import lax
from jax.experimental import pallas as pl
from jax.experimental.pallas import tpu as pltpu
from jax.sharding import PartitionSpec as P

GROUP = 4
BLOCKS = 2
STEP = GROUP * BLOCKS
SIDE = 3
EDGE = 16
MESH = pl.DeviceIdType.MESH


def lanczos(x):
    inside = jnp.abs(x) < 3.0
    u = jnp.where(inside, x, 0.0) * (math.pi / 3.0)
    square = u * u
    q = jnp.full_like(square, -1.0 / math.factorial(23))
    for k in range(10, -1, -1):
        q = q * square + (-1.0 if k % 2 else 1.0) / math.factorial(2 * k + 1)
    q2 = q * q
    return jnp.where(inside, q2 * (1.0 - (4.0 / 3.0) * square * q2), 0.0)


def tap_columns(padded, shift, width):
    sub = lax.broadcasted_iota(jnp.int32, (8, shift.shape[1]), 0)
    w = lanczos((sub - SIDE).astype(jnp.float32) - shift)
    w = jnp.where(sub <= 2 * SIDE, w, 0.0)
    w = w / jnp.sum(w, axis=0, keepdims=True)
    w = w.astype(jnp.bfloat16).astype(jnp.float32)
    terms = [
        w[m + SIDE : m + SIDE + 1] * padded[SIDE - m : SIDE - m + width, :]
        for m in range(-SIDE, SIDE + 1)
    ]
    down = terms[6] + terms[5] + terms[4]
    first = []
    for m in range(SIDE, -1, -1):
        down = down + terms[m]
        first.append(down)
    up = terms[0] + terms[1] + terms[2]
    last = []
    for m in range(SIDE, 2 * SIDE):
        up = up + terms[m]
        last.append(up)
    return first, last


def spread(ref, p, size):
    return [jnp.broadcast_to(ref[v, pl.ds(p, 1), :], (8, size)) for v in range(7)]


def turn(x, shift, size):
    return pltpu.roll(x, shift % size, 1, stride=1, stride_axis=0)


def assemble(base, top, second, before, end, keep, size):
    tiles = size // 8
    head = [jnp.where(keep[0], top, 0.0), jnp.where(keep[1], second, 0.0)]
    tail = [jnp.where(keep[tiles - 2], before, 0.0), jnp.where(keep[tiles - 1], end, 0.0)]
    pair = jnp.concatenate([base, pltpu.roll(base, 8, 1)], axis=0).astype(jnp.bfloat16)
    parts = [jnp.concatenate(head, axis=0).astype(jnp.bfloat16)]
    for v in range(1, tiles // 2 - 1):
        parts.append(pltpu.roll(pair, 16 * v, 1))
    parts.append(jnp.concatenate(tail, axis=0).astype(jnp.bfloat16))
    return parts


def row_band(ref, p, size, sub, keep):
    row = spread(ref, p, size)
    top = jnp.where(sub == 0, row[0], jnp.where(sub == 1, row[1], jnp.where(sub == 2, row[2], row[3])))
    end = jnp.where(sub == 7, row[4], jnp.where(sub == 6, row[5], jnp.where(sub == 5, row[6], row[3])))
    base = turn(row[3], 0, size)
    return assemble(
        base, turn(top, 0, size), pltpu.roll(base, 8, 1), pltpu.roll(base, size - 16, 1),
        turn(end, size - 8, size), keep, size,
    )


def column_band(ref, p, size, spots, keep):
    row = spread(ref, p, size)

    def edged(tile, three):
        x = row[3]
        for i in range(3):
            x = jnp.where(spots[tile, i], row[three + i], x)
        return turn(x, 8 * tile, size)

    last = size // 8 - 1
    return assemble(
        turn(row[3], 0, size), edged(0, 0), edged(1, 0), edged(last - 1, 4), edged(last, 4),
        keep, size,
    )


def sums_kernel(
    tile_hbm, visit_hbm, calib_hbm, weights_hbm, gain_ref, words_hbm, taps_hbm, shifts_hbm, pieces_ref,
    out_ref, gain_out,
    pbuf, words_ref, taps_ref, shifts_ref, padded, columns, left_taps, right_taps, good,
    acc, dacc, lbuf, rbuf, ibuf, cbuf,
    tile_ref, visit_ref, calib_ref, weights_ref, slots, blk_tile, cnt, cur, sems, small_sems,
):
    count, size, _ = pieces_ref.shape
    tiles = acc.shape[0]
    chunks = sems.shape[0]
    each = count // chunks
    smalls = [
        pltpu.make_async_copy(src, dst, small_sems.at[i])
        for i, (src, dst) in enumerate(
            (
                (tile_hbm, tile_ref), (shifts_hbm, shifts_ref), (taps_hbm, taps_ref),
                (words_hbm, words_ref), (visit_hbm, visit_ref), (calib_hbm, calib_ref),
                (weights_hbm, weights_ref),
            )
        )
    ]
    for copy in smalls:
        copy.start()
    copies = [
        pltpu.make_async_copy(
            pieces_ref.at[pl.ds(c * each, each)], pbuf.at[pl.ds(c * each, each)], sems.at[c]
        )
        for c in range(chunks)
    ]
    for copy in copies:
        copy.start()

    def clear_slot(i, carry):
        slots[i] = -1
        return carry

    lax.fori_loop(0, slots.shape[0], clear_slot, 0, unroll=8)

    def clear_blk(i, carry):
        blk_tile[i] = 0
        return carry

    lax.fori_loop(0, blk_tile.shape[0], clear_blk, 0, unroll=8)
    for t in range(tiles):
        cnt[t] = 0
        cur[t] = 0
        acc[t] = jnp.zeros((size, size), jnp.float32)
        dacc[t] = jnp.zeros((2 * EDGE, size), jnp.float32)
    lbuf[...] = jnp.zeros_like(lbuf)
    ibuf[...] = jnp.zeros_like(ibuf)
    cbuf[...] = jnp.zeros_like(cbuf)
    padded[...] = jnp.zeros_like(padded)
    for copy in smalls:
        copy.wait()

    gain_out[...] = jnp.full(gain_out.shape, gain_ref[0])

    def place(i, used):
        t = tile_ref[0, i]
        n = cnt[t]
        inside = n & (GROUP - 1)
        fresh = inside == 0
        b = jnp.where(fresh, used, cur[t])
        cur[t] = b
        blk_tile[b + BLOCKS] = t
        slots[b * GROUP + inside] = i
        cnt[t] = n + 1
        return jnp.where(fresh, used + 1, used)

    used = jnp.int32(0)
    for i in range(count):
        used = place(i, used)

    taps_count = taps_ref.shape[0]
    reach = (taps_count - 1) // 2 + SIDE
    block = size // 4
    wide = padded.shape[2]
    place_lane = lax.broadcasted_iota(jnp.int32, (size, size), 1)
    inside = (place_lane < block - reach) | (place_lane >= size - reach)
    for d, table in ((0, left_taps), (1, right_taps)):
        taps = taps_ref[:, d, :]
        if d == 1:
            taps = jnp.concatenate(
                [taps[t : t + 1, :] for t in range(taps_count - 1, -1, -1)], axis=0
            )
        kernel = taps / jnp.sum(taps, axis=0, keepdims=True)
        kernel = kernel.astype(jnp.bfloat16).astype(jnp.float32)
        padded[d, 2 * SIDE : 2 * SIDE + taps_count, 0:count] = kernel
        shift = jnp.concatenate(
            [shifts_ref[d : d + 1, :], jnp.zeros((1, wide - count), jnp.float32)], axis=1
        )
        if d == 0:
            first, last = tap_columns(padded.at[d], shift, block)
        else:
            last, first = tap_columns(padded.at[d], -shift, block)
            first, last = first + last[3:], last[:3]
        for v, rows in enumerate(first):
            columns[0, block * v : block * (v + 1), :] = rows
        for v, rows in enumerate(last):
            columns[1, block * v : block * (v + 1), :] = rows
        columns[1, 3 * block : size, :] = first[3]
        for h in range(2):
            for c in range(wide // size):
                part = columns[h, :, c * size : (c + 1) * size]
                turned = part.T
                for v in range(4 if h == 0 else 3):
                    x = pltpu.roll(turned, (-block * v - reach) % size, 1)
                    table[4 * h + v, c * size : (c + 1) * size, :] = jnp.where(inside, x, 0.0)
    bit = lax.broadcasted_iota(jnp.int32, (32, count), 0)
    flags = [
        (lax.shift_right_logical(jnp.broadcast_to(words_ref[k : k + 1, :], (32, count)), bit) & 1)
        for k in range(size // 32)
    ]
    columns[0, :, 0:count] = jnp.concatenate(flags, axis=0).astype(jnp.float32)
    for c in range(wide // size):
        good[c * size : (c + 1) * size, :] = columns[0, :, c * size : (c + 1) * size].T

    sub = lax.broadcasted_iota(jnp.int32, (8, size), 0)
    lane = lax.broadcasted_iota(jnp.int32, (8, size), 1)
    final = size // 8 - 1
    keep = {v: jnp.abs(lane - sub - 8 * v) <= reach for v in (0, 1, final - 1, final)}
    spots = {}
    for tile in (0, 1):
        for i in range(3):
            spots[tile, i] = lane == ((i - sub - 8 * tile) & (size - 1))
    for tile in (final - 1, final):
        for i in range(3):
            spots[tile, i] = lane == ((size - 1 - i - sub - 8 * tile) & (size - 1))

    def piece_of(step, g):
        return jnp.maximum(slots[step * STEP + g], 0)

    def weight_of(step, g):
        p = slots[step * STEP + g]
        v = visit_ref[0, jnp.maximum(p, 0)]
        w = jnp.where(p >= 0, weights_ref[0, v], 0).astype(jnp.float32)
        return w, w * calib_ref[0, v]

    def build_right(step, g):
        parts = column_band(right_taps, piece_of(step, g), size, spots, keep)
        for v, part in enumerate(parts):
            rbuf[g, 16 * v : 16 * v + 16, :] = part

    def build_left(step, g):
        parts = row_band(left_taps, piece_of(step, g), size, sub, keep)
        for v, part in enumerate(parts):
            lbuf[16 * v : 16 * v + 16, g * size : (g + 1) * size] = part

    for g in range(STEP):
        build_right(0, g)
    for copy in copies:
        copy.wait()

    def add_up(k):
        for j in range(BLOCKS):
            t = blk_tile[k * BLOCKS + j]
            here = slice(j * GROUP * size, (j + 1) * GROUP * size)
            part = jnp.dot(lbuf[:, here], ibuf[here, :], preferred_element_type=jnp.float32)
            acc[t] = acc[t] + part
            den = dacc[t]
            for g in range(j * GROUP, (j + 1) * GROUP):
                cols = slice(g * size, (g + 1) * size)
                rim = jnp.concatenate(
                    [lbuf[0:EDGE, cols], lbuf[size - EDGE : size, cols]], axis=0
                ).astype(jnp.float32)
                den = den + jnp.sum(rim, axis=1, keepdims=True) * cbuf[g, 0:1, :]
            dacc[t] = den

    def step_body(k, carry):
        add_up(k)
        for g in range(STEP):
            p = piece_of(k, g)
            w, factor = weight_of(k, g)
            mask = jnp.broadcast_to(good[pl.ds(p, 1), :], (16, size)).astype(jnp.bfloat16)
            rows = [pbuf[p, 16 * v : 16 * v + 16, :] * mask for v in range(size // 16)]
            x = jnp.concatenate(rows + [mask], axis=0)
            y = jnp.dot(x, rbuf[g], preferred_element_type=jnp.float32)
            ibuf[g * size : (g + 1) * size, :] = (y[0:size] * factor).astype(jnp.bfloat16)
            cbuf[g] = y[size : size + 8] * w
            build_left(k, g)
            build_right(k + 1, g)
        return carry

    steps = (used + (BLOCKS - 1)) // BLOCKS
    lax.fori_loop(0, steps, step_body, 0)
    add_up(steps)
    for t in range(tiles):
        out_ref[t, 0:size, :] = acc[t].astype(jnp.bfloat16)
        out_ref[t, size : size + 2 * EDGE, :] = dacc[t].astype(jnp.bfloat16)


def local_sums(pieces, visit, tile, words, taps, shifts, calib, weights, gain, tiles):
    count, size, _ = pieces.shape
    blocks = (count + tiles * (GROUP - 1)) // GROUP
    blocks = (-(-blocks // BLOCKS) + 2) * BLOCKS
    hbm = pl.BlockSpec(memory_space=pltpu.HBM)
    chunks = 8 if count % 8 == 0 else 1
    wide = -(-count // size) * size
    return pl.pallas_call(
        sums_kernel,
        out_shape=(
            jax.ShapeDtypeStruct((tiles, size + 2 * EDGE, size), jnp.bfloat16),
            jax.ShapeDtypeStruct((8, size), jnp.float32),
        ),
        in_specs=[hbm] * 4 + [pl.BlockSpec(memory_space=pltpu.SMEM)] + [hbm] * 4,
        out_specs=(pl.BlockSpec(memory_space=pltpu.VMEM),) * 2,
        scratch_shapes=[
            pltpu.VMEM((count, size, size), jnp.bfloat16),
            pltpu.VMEM(words.shape, jnp.int32),
            pltpu.VMEM(taps.shape, jnp.float32),
            pltpu.VMEM(shifts.shape, jnp.float32),
            pltpu.VMEM((2, size // 4 + 8, wide), jnp.float32),
            pltpu.VMEM((2, size, wide), jnp.float32),
            pltpu.VMEM((7, wide, size), jnp.float32),
            pltpu.VMEM((7, wide, size), jnp.float32),
            pltpu.VMEM((wide, size), jnp.float32),
            pltpu.VMEM((tiles, size, size), jnp.float32),
            pltpu.VMEM((tiles, 2 * EDGE, size), jnp.float32),
            pltpu.VMEM((size, STEP * size), jnp.bfloat16),
            pltpu.VMEM((STEP, size, size), jnp.bfloat16),
            pltpu.VMEM((STEP * size, size), jnp.bfloat16),
            pltpu.VMEM((STEP, 8, size), jnp.float32),
            pltpu.SMEM(tile.shape, jnp.int32),
            pltpu.SMEM(visit.shape, jnp.int32),
            pltpu.SMEM(calib.shape, jnp.float32),
            pltpu.SMEM(weights.shape, jnp.int32),
            pltpu.SMEM((blocks * GROUP,), jnp.int32),
            pltpu.SMEM((blocks + BLOCKS,), jnp.int32),
            pltpu.SMEM((tiles,), jnp.int32),
            pltpu.SMEM((tiles,), jnp.int32),
            pltpu.SemaphoreType.DMA((chunks,)),
            pltpu.SemaphoreType.DMA((7,)),
        ],
        compiler_params=pltpu.CompilerParams(vmem_limit_bytes=56 * 1024 * 1024),
        name="local_sums",
    )(tile, visit, calib, weights, gain, words, taps, shifts, pieces)


def owner_kernel(
    owners, bands, gain_ref, sums_ref, coadd_ref, det_ref,
    own, near, pair, far, mine, other, gain, gain_sem, own_sem,
    near_send, near_recv, far_send, far_recv, band_send, band_recv,
):
    size = coadd_ref.shape[0]
    half = owners // 2
    me = lax.axis_index("vis")
    band = lax.axis_index("band")
    mate = me + 1 - 2 * lax.rem(me, 2)
    load = pltpu.make_async_copy(gain_ref, gain, gain_sem)
    load.start()
    order = list(range(1, half)) + [0]
    fetch = {}
    for o in order:
        fetch[o] = pltpu.make_async_copy(
            sums_ref.at[lax.rem(me + 2 * o, owners)], own.at[o], own_sem.at[o]
        )
        fetch[o].start()
    barrier = pltpu.get_barrier_semaphore()
    pl.semaphore_signal(barrier, inc=1, device_id={"vis": mate}, device_id_type=MESH)
    for o in range(1, half):
        pl.semaphore_signal(
            barrier, inc=1, device_id={"vis": lax.rem(me + 2 * o, owners)}, device_id_type=MESH
        )
    for o in range(1, bands):
        pl.semaphore_signal(
            barrier, inc=1, device_id={"band": lax.rem(band + o, bands)}, device_id_type=MESH
        )
    pl.semaphore_wait(barrier, half + bands - 1)
    nears, fars = {}, {}
    for o in order:
        nears[o] = pltpu.make_async_remote_copy(
            src_ref=sums_ref.at[lax.rem(mate + 2 * o, owners)],
            dst_ref=near.at[o],
            send_sem=near_send.at[o],
            recv_sem=near_recv.at[o],
            device_id={"vis": mate},
            device_id_type=MESH,
        )
        nears[o].start()
    total = None
    for o in order:
        fetch[o].wait()
        nears[o].wait_recv()
        both = own[o].astype(jnp.float32) + near[o].astype(jnp.float32)
        if o == 0:
            total = both
            continue
        pair[o] = both.astype(jnp.bfloat16)
        fars[o] = pltpu.make_async_remote_copy(
            src_ref=pair.at[o],
            dst_ref=far.at[o],
            send_sem=far_send.at[o],
            recv_sem=far_recv.at[o],
            device_id={"vis": lax.rem(me + 2 * o, owners)},
            device_id_type=MESH,
        )
        fars[o].start()
    for o in range(1, half):
        fars[o].wait_recv()
        total = total + far[o].astype(jnp.float32)
    num = total[0:size]
    rim = jnp.maximum(total[size:], 1.0)
    inner = jnp.broadcast_to(rim[EDGE - 1 : EDGE], (size - 2 * EDGE, size))
    den = jnp.concatenate([rim[:EDGE], inner, rim[EDGE:]], axis=0)
    coadd = num / den
    coadd_ref[...] = coadd
    load.wait()
    scaled = coadd * gain[0:1, :]
    mine[...] = scaled
    swaps = []
    for o in range(1, bands):
        swap = pltpu.make_async_remote_copy(
            src_ref=mine,
            dst_ref=other.at[o],
            send_sem=band_send.at[o],
            recv_sem=band_recv.at[o],
            device_id={"band": lax.rem(band + o, bands)},
            device_id_type=MESH,
        )
        swap.start()
        swaps.append(swap)
    for o in range(1, bands):
        swaps[o - 1].wait_recv()
        scaled = scaled + other[o]
    det_ref[...] = scaled
    for copy in list(nears.values()) + list(fars.values()) + swaps:
        copy.wait_send()


def owner_coadd(gain, sums, owners, bands):
    tiles, rows, size = sums.shape
    half = owners // 2
    vmem = pl.BlockSpec(memory_space=pltpu.VMEM)
    out = jax.ShapeDtypeStruct((size, size), jnp.float32)
    return pl.pallas_call(
        functools.partial(owner_kernel, owners, bands),
        out_shape=(out, out),
        in_specs=[pl.BlockSpec(memory_space=pltpu.HBM)] * 2,
        out_specs=(vmem, vmem),
        scratch_shapes=[
            pltpu.VMEM((half, rows, size), jnp.bfloat16),
            pltpu.VMEM((half, rows, size), jnp.bfloat16),
            pltpu.VMEM((half, rows, size), jnp.bfloat16),
            pltpu.VMEM((half, rows, size), jnp.bfloat16),
            pltpu.VMEM((size, size), jnp.float32),
            pltpu.VMEM((bands, size, size), jnp.float32),
            pltpu.VMEM(gain.shape, jnp.float32),
            pltpu.SemaphoreType.DMA,
            pltpu.SemaphoreType.DMA((half,)),
            pltpu.SemaphoreType.DMA((half,)),
            pltpu.SemaphoreType.DMA((half,)),
            pltpu.SemaphoreType.DMA((half,)),
            pltpu.SemaphoreType.DMA((half,)),
            pltpu.SemaphoreType.DMA((bands,)),
            pltpu.SemaphoreType.DMA((bands,)),
        ],
        compiler_params=pltpu.CompilerParams(
            collective_id=0, has_side_effects=True, vmem_limit_bytes=56 * 1024 * 1024
        ),
        name="owner_coadd",
    )(gain, sums)


def write_kernel(coadd_ref, det_ref, coadd_out, det_out):
    coadd_out[...] = coadd_ref[...]
    det_out[...] = det_ref[...]


def write_out(coadd, detection):
    vmem = pl.BlockSpec(memory_space=pltpu.VMEM)
    out = jax.ShapeDtypeStruct(coadd.shape, coadd.dtype)
    return pl.pallas_call(
        write_kernel,
        out_shape=(out, out),
        in_specs=[vmem, vmem],
        out_specs=(vmem, vmem),
        compiler_params=pltpu.CompilerParams(vmem_limit_bytes=56 * 1024 * 1024),
        name="write_out",
    )(coadd, detection)


def shards(pieces, visit, tile_map, good_columns, psf_taps, shifts, calib, weights, band_gain):
    owners = lax.axis_size("vis")
    sums, gain = local_sums(
        pieces[0], visit, tile_map[:, :, 0], good_columns[0].T, psf_taps[0].transpose(2, 1, 0),
        shifts[0].T, calib, weights, band_gain, owners,
    )
    coadd, detection = owner_coadd(gain, sums, owners, lax.axis_size("band"))
    coadd, detection = write_out(coadd, detection)
    return (coadd[None], detection)


def solution(mesh):
    placed = (
        P("band", ("groups", "vis"), None, None),
        P("band", ("groups", "vis")),
        P("band", ("groups", "vis"), None),
        P("band", ("groups", "vis"), None),
        P("band", ("groups", "vis"), None, None),
        P("band", ("groups", "vis"), None),
        P("band", None),
        P("band", None),
        P("band"),
    )
    return jax.shard_map(
        shards,
        mesh=mesh,
        in_specs=placed,
        out_specs=(P("band", ("groups", "vis"), None), P(("groups", "vis"), None)),
        check_vma=False,
    )
```

```python
import functools
import math

import jax
import jax.numpy as jnp
from jax import lax
from jax.experimental import pallas as pl
from jax.experimental.pallas import tpu as pltpu
from jax.sharding import PartitionSpec as P

GROUP = 4
BLOCKS = 2
STEP = GROUP * BLOCKS
SIDE = 3
EDGE = 16
MESH = pl.DeviceIdType.MESH


def lanczos(x):
    inside = jnp.abs(x) < 3.0
    u = jnp.where(inside, x, 0.0) * (math.pi / 3.0)
    square = u * u
    q = jnp.full_like(square, -1.0 / math.factorial(23))
    for k in range(10, -1, -1):
        q = q * square + (-1.0 if k % 2 else 1.0) / math.factorial(2 * k + 1)
    q2 = q * q
    return jnp.where(inside, q2 * (1.0 - (4.0 / 3.0) * square * q2), 0.0)


def tap_columns(padded, shift, width):
    sub = lax.broadcasted_iota(jnp.int32, (8, shift.shape[1]), 0)
    w = lanczos((sub - SIDE).astype(jnp.float32) - shift)
    w = jnp.where(sub <= 2 * SIDE, w, 0.0)
    w = w / jnp.sum(w, axis=0, keepdims=True)
    w = w.astype(jnp.bfloat16).astype(jnp.float32)
    terms = [
        w[m + SIDE : m + SIDE + 1] * padded[SIDE - m : SIDE - m + width, :]
        for m in range(-SIDE, SIDE + 1)
    ]
    down = terms[6] + terms[5] + terms[4]
    first = []
    for m in range(SIDE, -1, -1):
        down = down + terms[m]
        first.append(down)
    up = terms[0] + terms[1] + terms[2]
    last = []
    for m in range(SIDE, 2 * SIDE):
        up = up + terms[m]
        last.append(up)
    return first, last


def spread(ref, p, size):
    return [jnp.broadcast_to(ref[v, pl.ds(p, 1), :], (8, size)) for v in range(7)]


def turn(x, shift, size):
    return pltpu.roll(x, shift % size, 1, stride=1, stride_axis=0)


def assemble(base, top, second, before, end, keep, size):
    tiles = size // 8
    head = [jnp.where(keep[0], top, 0.0), jnp.where(keep[1], second, 0.0)]
    tail = [jnp.where(keep[tiles - 2], before, 0.0), jnp.where(keep[tiles - 1], end, 0.0)]
    pair = jnp.concatenate([base, pltpu.roll(base, 8, 1)], axis=0).astype(jnp.bfloat16)
    parts = [jnp.concatenate(head, axis=0).astype(jnp.bfloat16)]
    for v in range(1, tiles // 2 - 1):
        parts.append(pltpu.roll(pair, 16 * v, 1))
    parts.append(jnp.concatenate(tail, axis=0).astype(jnp.bfloat16))
    return parts


def row_band(ref, p, size, sub, keep):
    row = spread(ref, p, size)
    top = jnp.where(sub == 0, row[0], jnp.where(sub == 1, row[1], jnp.where(sub == 2, row[2], row[3])))
    end = jnp.where(sub == 7, row[4], jnp.where(sub == 6, row[5], jnp.where(sub == 5, row[6], row[3])))
    base = turn(row[3], 0, size)
    return assemble(
        base, turn(top, 0, size), pltpu.roll(base, 8, 1), pltpu.roll(base, size - 16, 1),
        turn(end, size - 8, size), keep, size,
    )


def column_band(ref, p, size, spots, keep):
    row = spread(ref, p, size)

    def edged(tile, three):
        x = row[3]
        for i in range(3):
            x = jnp.where(spots[tile, i], row[three + i], x)
        return turn(x, 8 * tile, size)

    last = size // 8 - 1
    return assemble(
        turn(row[3], 0, size), edged(0, 0), edged(1, 0), edged(last - 1, 4), edged(last, 4),
        keep, size,
    )


def sums_kernel(
    tile_hbm, visit_hbm, calib_hbm, weights_hbm, gain_ref, words_hbm, taps_hbm, shifts_hbm, pieces_ref,
    out_ref, gain_out,
    pbuf, words_ref, taps_ref, shifts_ref, padded, columns, left_taps, right_taps, good,
    acc, dacc, lbuf, rbuf, ibuf, cbuf,
    tile_ref, visit_ref, calib_ref, weights_ref, slots, blk_tile, cnt, cur, sems, small_sems,
):
    count, size, _ = pieces_ref.shape
    tiles = acc.shape[0]
    chunks = sems.shape[0]
    each = count // chunks
    smalls = [
        pltpu.make_async_copy(src, dst, small_sems.at[i])
        for i, (src, dst) in enumerate(
            (
                (tile_hbm, tile_ref), (shifts_hbm, shifts_ref), (taps_hbm, taps_ref),
                (words_hbm, words_ref), (visit_hbm, visit_ref), (calib_hbm, calib_ref),
                (weights_hbm, weights_ref),
            )
        )
    ]
    for copy in smalls:
        copy.start()
    copies = [
        pltpu.make_async_copy(
            pieces_ref.at[pl.ds(c * each, each)], pbuf.at[pl.ds(c * each, each)], sems.at[c]
        )
        for c in range(chunks)
    ]
    for copy in copies:
        copy.start()

    def clear_slot(i, carry):
        slots[i] = -1
        return carry

    lax.fori_loop(0, slots.shape[0], clear_slot, 0, unroll=8)

    def clear_blk(i, carry):
        blk_tile[i] = 0
        return carry

    lax.fori_loop(0, blk_tile.shape[0], clear_blk, 0, unroll=8)
    for t in range(tiles):
        cnt[t] = 0
        cur[t] = 0
        acc[t] = jnp.zeros((size, size), jnp.float32)
        dacc[t] = jnp.zeros((2 * EDGE, size), jnp.float32)
    lbuf[...] = jnp.zeros_like(lbuf)
    ibuf[...] = jnp.zeros_like(ibuf)
    rbuf[...] = jnp.zeros_like(rbuf)
    cbuf[...] = jnp.zeros_like(cbuf)
    padded[...] = jnp.zeros_like(padded)
    for copy in smalls:
        copy.wait()

    gain_out[...] = jnp.full(gain_out.shape, gain_ref[0])

    def place(i, used):
        t = tile_ref[0, i]
        n = cnt[t]
        inside = n & (GROUP - 1)
        fresh = inside == 0
        b = jnp.where(fresh, used, cur[t])
        cur[t] = b
        blk_tile[b + BLOCKS] = t
        slots[b * GROUP + inside] = i
        cnt[t] = n + 1
        return jnp.where(fresh, used + 1, used)

    used = jnp.int32(0)
    for i in range(count):
        used = place(i, used)

    taps_count = taps_ref.shape[0]
    reach = (taps_count - 1) // 2 + SIDE
    block = size // 4
    wide = padded.shape[2]
    place_lane = lax.broadcasted_iota(jnp.int32, (size, size), 1)
    inside = (place_lane < block - reach) | (place_lane >= size - reach)
    for d, table in ((0, left_taps), (1, right_taps)):
        taps = taps_ref[:, d, :]
        if d == 1:
            taps = jnp.concatenate(
                [taps[t : t + 1, :] for t in range(taps_count - 1, -1, -1)], axis=0
            )
        kernel = taps / jnp.sum(taps, axis=0, keepdims=True)
        kernel = kernel.astype(jnp.bfloat16).astype(jnp.float32)
        padded[d, 2 * SIDE : 2 * SIDE + taps_count, 0:count] = kernel
        shift = jnp.concatenate(
            [shifts_ref[d : d + 1, :], jnp.zeros((1, wide - count), jnp.float32)], axis=1
        )
        if d == 0:
            first, last = tap_columns(padded.at[d], shift, block)
        else:
            last, first = tap_columns(padded.at[d], -shift, block)
            first, last = first + last[3:], last[:3]
        for v, rows in enumerate(first):
            columns[0, block * v : block * (v + 1), :] = rows
        for v, rows in enumerate(last):
            columns[1, block * v : block * (v + 1), :] = rows
        columns[1, 3 * block : size, :] = first[3]
        for h in range(2):
            for c in range(wide // size):
                part = columns[h, :, c * size : (c + 1) * size]
                turned = part.T
                for v in range(4 if h == 0 else 3):
                    x = pltpu.roll(turned, (-block * v - reach) % size, 1)
                    table[4 * h + v, c * size : (c + 1) * size, :] = jnp.where(inside, x, 0.0)
    bit = lax.broadcasted_iota(jnp.int32, (32, count), 0)
    flags = [
        (lax.shift_right_logical(jnp.broadcast_to(words_ref[k : k + 1, :], (32, count)), bit) & 1)
        for k in range(size // 32)
    ]
    columns[0, :, 0:count] = jnp.concatenate(flags, axis=0).astype(jnp.float32)
    for c in range(wide // size):
        good[c * size : (c + 1) * size, :] = columns[0, :, c * size : (c + 1) * size].T

    sub = lax.broadcasted_iota(jnp.int32, (8, size), 0)
    lane = lax.broadcasted_iota(jnp.int32, (8, size), 1)
    final = size // 8 - 1
    keep = {v: jnp.abs(lane - sub - 8 * v) <= reach for v in (0, 1, final - 1, final)}
    spots = {}
    for tile in (0, 1):
        for i in range(3):
            spots[tile, i] = lane == ((i - sub - 8 * tile) & (size - 1))
    for tile in (final - 1, final):
        for i in range(3):
            spots[tile, i] = lane == ((size - 1 - i - sub - 8 * tile) & (size - 1))

    def piece_of(step, g):
        return jnp.maximum(slots[step * STEP + g], 0)

    def weight_of(step, g):
        p = slots[step * STEP + g]
        v = visit_ref[0, jnp.maximum(p, 0)]
        w = jnp.where(p >= 0, weights_ref[0, v], 0).astype(jnp.float32)
        return w, w * calib_ref[0, v]

    def build_right(step, g):
        parts = column_band(right_taps, piece_of(step, g), size, spots, keep)
        for v, part in enumerate(parts):
            here = size * (g % 2)
            rbuf[g // 2, here + 16 * v : here + 16 * v + 16, here : here + size] = part

    def build_left(step, g):
        parts = row_band(left_taps, piece_of(step, g), size, sub, keep)
        for v, part in enumerate(parts):
            lbuf[16 * v : 16 * v + 16, g * size : (g + 1) * size] = part

    for g in range(STEP):
        build_right(0, g)
    for copy in copies:
        copy.wait()

    def add_up(k):
        for j in range(BLOCKS):
            t = blk_tile[k * BLOCKS + j]
            here = slice(j * GROUP * size, (j + 1) * GROUP * size)
            part = jnp.dot(lbuf[:, here], ibuf[here, :], preferred_element_type=jnp.float32)
            acc[t] = acc[t] + part
            den = dacc[t]
            for g in range(j * GROUP, (j + 1) * GROUP):
                cols = slice(g * size, (g + 1) * size)
                rim = jnp.concatenate(
                    [lbuf[0:EDGE, cols], lbuf[size - EDGE : size, cols]], axis=0
                ).astype(jnp.float32)
                den = den + jnp.sum(rim, axis=1, keepdims=True) * cbuf[g, 0:1, :]
            dacc[t] = den

    def step_body(k, carry):
        add_up(k)
        for first in range(0, STEP, 2):
            sides = []
            for g in (first, first + 1):
                p = piece_of(k, g)
                mask = jnp.broadcast_to(good[pl.ds(p, 1), :], (16, size)).astype(jnp.bfloat16)
                rows = [pbuf[p, 16 * v : 16 * v + 16, :] * mask for v in range(size // 16)]
                sides.append(jnp.concatenate(rows + [mask], axis=0))
            x = jnp.concatenate(sides, axis=1)
            both = jnp.dot(x, rbuf[first // 2], preferred_element_type=jnp.float32)
            for g in (first, first + 1):
                w, factor = weight_of(k, g)
                y = both[:, size * (g - first) : size * (g - first + 1)]
                ibuf[g * size : (g + 1) * size, :] = (y[0:size] * factor).astype(jnp.bfloat16)
                cbuf[g] = y[size : size + 8] * w
                build_left(k, g)
                build_right(k + 1, g)
        return carry

    steps = (used + (BLOCKS - 1)) // BLOCKS
    lax.fori_loop(0, steps, step_body, 0)
    add_up(steps)
    for t in range(tiles):
        out_ref[t, 0:size, :] = acc[t].astype(jnp.bfloat16)
        out_ref[t, size : size + 2 * EDGE, :] = dacc[t].astype(jnp.bfloat16)


def local_sums(pieces, visit, tile, words, taps, shifts, calib, weights, gain, tiles):
    count, size, _ = pieces.shape
    blocks = (count + tiles * (GROUP - 1)) // GROUP
    blocks = (-(-blocks // BLOCKS) + 2) * BLOCKS
    hbm = pl.BlockSpec(memory_space=pltpu.HBM)
    chunks = 8 if count % 8 == 0 else 1
    wide = -(-count // size) * size
    return pl.pallas_call(
        sums_kernel,
        out_shape=(
            jax.ShapeDtypeStruct((tiles, size + 2 * EDGE, size), jnp.bfloat16),
            jax.ShapeDtypeStruct((8, size), jnp.float32),
        ),
        in_specs=[hbm] * 4 + [pl.BlockSpec(memory_space=pltpu.SMEM)] + [hbm] * 4,
        out_specs=(pl.BlockSpec(memory_space=pltpu.VMEM),) * 2,
        scratch_shapes=[
            pltpu.VMEM((count, size, size), jnp.bfloat16),
            pltpu.VMEM(words.shape, jnp.int32),
            pltpu.VMEM(taps.shape, jnp.float32),
            pltpu.VMEM(shifts.shape, jnp.float32),
            pltpu.VMEM((2, size // 4 + 8, wide), jnp.float32),
            pltpu.VMEM((2, size, wide), jnp.float32),
            pltpu.VMEM((7, wide, size), jnp.float32),
            pltpu.VMEM((7, wide, size), jnp.float32),
            pltpu.VMEM((wide, size), jnp.float32),
            pltpu.VMEM((tiles, size, size), jnp.float32),
            pltpu.VMEM((tiles, 2 * EDGE, size), jnp.float32),
            pltpu.VMEM((size, STEP * size), jnp.bfloat16),
            pltpu.VMEM((STEP // 2, 2 * size, 2 * size), jnp.bfloat16),
            pltpu.VMEM((STEP * size, size), jnp.bfloat16),
            pltpu.VMEM((STEP, 8, size), jnp.float32),
            pltpu.SMEM(tile.shape, jnp.int32),
            pltpu.SMEM(visit.shape, jnp.int32),
            pltpu.SMEM(calib.shape, jnp.float32),
            pltpu.SMEM(weights.shape, jnp.int32),
            pltpu.SMEM((blocks * GROUP,), jnp.int32),
            pltpu.SMEM((blocks + BLOCKS,), jnp.int32),
            pltpu.SMEM((tiles,), jnp.int32),
            pltpu.SMEM((tiles,), jnp.int32),
            pltpu.SemaphoreType.DMA((chunks,)),
            pltpu.SemaphoreType.DMA((7,)),
        ],
        compiler_params=pltpu.CompilerParams(vmem_limit_bytes=56 * 1024 * 1024),
        name="local_sums",
    )(tile, visit, calib, weights, gain, words, taps, shifts, pieces)


def owner_kernel(
    owners, bands, gain_ref, sums_ref, coadd_ref, det_ref,
    own, near, pair, far, mine, other, gain, gain_sem, own_sem,
    near_send, near_recv, far_send, far_recv, band_send, band_recv,
):
    size = coadd_ref.shape[0]
    half = owners // 2
    me = lax.axis_index("vis")
    band = lax.axis_index("band")
    mate = me + 1 - 2 * lax.rem(me, 2)
    load = pltpu.make_async_copy(gain_ref, gain, gain_sem)
    load.start()
    order = list(range(1, half)) + [0]
    fetch = {}
    for o in order:
        fetch[o] = pltpu.make_async_copy(
            sums_ref.at[lax.rem(me + 2 * o, owners)], own.at[o], own_sem.at[o]
        )
        fetch[o].start()
    barrier = pltpu.get_barrier_semaphore()
    pl.semaphore_signal(barrier, inc=1, device_id={"vis": mate}, device_id_type=MESH)
    for o in range(1, half):
        pl.semaphore_signal(
            barrier, inc=1, device_id={"vis": lax.rem(me + 2 * o, owners)}, device_id_type=MESH
        )
    for o in range(1, bands):
        pl.semaphore_signal(
            barrier, inc=1, device_id={"band": lax.rem(band + o, bands)}, device_id_type=MESH
        )
    pl.semaphore_wait(barrier, half + bands - 1)
    nears, fars = {}, {}
    for o in order:
        nears[o] = pltpu.make_async_remote_copy(
            src_ref=sums_ref.at[lax.rem(mate + 2 * o, owners)],
            dst_ref=near.at[o],
            send_sem=near_send.at[o],
            recv_sem=near_recv.at[o],
            device_id={"vis": mate},
            device_id_type=MESH,
        )
        nears[o].start()
    total = None
    for o in order:
        fetch[o].wait()
        nears[o].wait_recv()
        both = own[o].astype(jnp.float32) + near[o].astype(jnp.float32)
        if o == 0:
            total = both
            continue
        pair[o] = both.astype(jnp.bfloat16)
        fars[o] = pltpu.make_async_remote_copy(
            src_ref=pair.at[o],
            dst_ref=far.at[o],
            send_sem=far_send.at[o],
            recv_sem=far_recv.at[o],
            device_id={"vis": lax.rem(me + 2 * o, owners)},
            device_id_type=MESH,
        )
        fars[o].start()
    for o in range(1, half):
        fars[o].wait_recv()
        total = total + far[o].astype(jnp.float32)
    num = total[0:size]
    rim = jnp.maximum(total[size:], 1.0)
    inner = jnp.broadcast_to(rim[EDGE - 1 : EDGE], (size - 2 * EDGE, size))
    den = jnp.concatenate([rim[:EDGE], inner, rim[EDGE:]], axis=0)
    coadd = num / den
    coadd_ref[...] = coadd
    load.wait()
    scaled = coadd * gain[0:1, :]
    mine[...] = scaled
    swaps = []
    for o in range(1, bands):
        swap = pltpu.make_async_remote_copy(
            src_ref=mine,
            dst_ref=other.at[o],
            send_sem=band_send.at[o],
            recv_sem=band_recv.at[o],
            device_id={"band": lax.rem(band + o, bands)},
            device_id_type=MESH,
        )
        swap.start()
        swaps.append(swap)
    for o in range(1, bands):
        swaps[o - 1].wait_recv()
        scaled = scaled + other[o]
    det_ref[...] = scaled
    for copy in list(nears.values()) + list(fars.values()) + swaps:
        copy.wait_send()


def owner_coadd(gain, sums, owners, bands):
    tiles, rows, size = sums.shape
    half = owners // 2
    vmem = pl.BlockSpec(memory_space=pltpu.VMEM)
    out = jax.ShapeDtypeStruct((size, size), jnp.float32)
    return pl.pallas_call(
        functools.partial(owner_kernel, owners, bands),
        out_shape=(out, out),
        in_specs=[pl.BlockSpec(memory_space=pltpu.HBM)] * 2,
        out_specs=(vmem, vmem),
        scratch_shapes=[
            pltpu.VMEM((half, rows, size), jnp.bfloat16),
            pltpu.VMEM((half, rows, size), jnp.bfloat16),
            pltpu.VMEM((half, rows, size), jnp.bfloat16),
            pltpu.VMEM((half, rows, size), jnp.bfloat16),
            pltpu.VMEM((size, size), jnp.float32),
            pltpu.VMEM((bands, size, size), jnp.float32),
            pltpu.VMEM(gain.shape, jnp.float32),
            pltpu.SemaphoreType.DMA,
            pltpu.SemaphoreType.DMA((half,)),
            pltpu.SemaphoreType.DMA((half,)),
            pltpu.SemaphoreType.DMA((half,)),
            pltpu.SemaphoreType.DMA((half,)),
            pltpu.SemaphoreType.DMA((half,)),
            pltpu.SemaphoreType.DMA((bands,)),
            pltpu.SemaphoreType.DMA((bands,)),
        ],
        compiler_params=pltpu.CompilerParams(
            collective_id=0, has_side_effects=True, vmem_limit_bytes=56 * 1024 * 1024
        ),
        name="owner_coadd",
    )(gain, sums)


def write_kernel(coadd_ref, det_ref, coadd_out, det_out):
    coadd_out[...] = coadd_ref[...]
    det_out[...] = det_ref[...]


def write_out(coadd, detection):
    vmem = pl.BlockSpec(memory_space=pltpu.VMEM)
    out = jax.ShapeDtypeStruct(coadd.shape, coadd.dtype)
    return pl.pallas_call(
        write_kernel,
        out_shape=(out, out),
        in_specs=[vmem, vmem],
        out_specs=(vmem, vmem),
        compiler_params=pltpu.CompilerParams(vmem_limit_bytes=56 * 1024 * 1024),
        name="write_out",
    )(coadd, detection)


def shards(pieces, visit, tile_map, good_columns, psf_taps, shifts, calib, weights, band_gain):
    owners = lax.axis_size("vis")
    sums, gain = local_sums(
        pieces[0], visit, tile_map[:, :, 0], good_columns[0].T, psf_taps[0].transpose(2, 1, 0),
        shifts[0].T, calib, weights, band_gain, owners,
    )
    coadd, detection = owner_coadd(gain, sums, owners, lax.axis_size("band"))
    coadd, detection = write_out(coadd, detection)
    return (coadd[None], detection)


def solution(mesh):
    placed = (
        P("band", ("groups", "vis"), None, None),
        P("band", ("groups", "vis")),
        P("band", ("groups", "vis"), None),
        P("band", ("groups", "vis"), None),
        P("band", ("groups", "vis"), None, None),
        P("band", ("groups", "vis"), None),
        P("band", None),
        P("band", None),
        P("band"),
    )
    return jax.shard_map(
        shards,
        mesh=mesh,
        in_specs=placed,
        out_specs=(P("band", ("groups", "vis"), None), P(("groups", "vis"), None)),
        check_vma=False,
    )
```
